32 devices in a mesh: queue: 8 (over y, x, core), head: 4 (over z).
Axes of the slice: x: 2, y: 2, z: 4, core: 2. Of those that a mesh axis runs over, the one named last changes fastest.
Arguments:
- latents: bfloat16 [16, 384, 5120], P('queue'), may hold values from -6 to 6
- control: bfloat16 [16, 384, 5120], P('queue'), may hold values from -3 to 3
- levels: int32 [16], P('queue'), may hold values from 0 to 63
- window_mask: int32 [16, 2], P('queue'), may hold values 0 or 1
- modulation: float32 [64, 3, 5120], replicated, may hold values from -3 to 3
- w_query: bfloat16 [5120, 2560], P('queue', 'head'), may hold values from -1 to 1
- w_key: bfloat16 [5120, 2560], P('queue', 'head'), may hold values from -1 to 1
- w_value: bfloat16 [5120, 2560], P('queue', 'head'), may hold values from -0.078125 to 0.078125
- w_out: bfloat16 [2560, 5120], P('head', 'queue'), may hold values from -0.125 to 0.125
- q_gain: float32 [2560], P('head'), may hold values from 0.6 to 8
- k_gain: float32 [2560], P('head'), may hold values from 0.6 to 8
Outputs:
- next_queue: float32 [16, 384, 5120], P('queue', None, 'head')
The draws below stay inside these ranges and needn't reach their ends.
All inputs are finite; a program needn't handle non-finite values. No bound on the sum of `window_mask` on one device may be relied on, other than what follows from the above.
Results may differ from the reference program's by a relative error of at most 0.019.
The reference program's roundings to bfloat16 on the way (of `normed`, `query`, `qhat`, `probs` and `attended`) count: a program that leaves them out, or rounds other values in their place, can miss the bound.
Values may be sent and summed in bfloat16 or wider, within the bound.
No kernel may reach another device: no remote copies, remote signals or barrier semaphores. Data moves between devices by JAX's collectives and lax.ppermute only.
A program may use at most 192 MiB of HBM per device.

```python
import jax
import jax.numpy as jnp
from jax import lax

D = 5120
HEADS = 20
HD = 128
ROWS = 384
LEVELS = 64
SPANS = 16
N_HEAD = 4


def column_scales(key, spread):
    columns = HEADS * HD
    position = jnp.arange(columns, dtype=jnp.float32) / (columns - 1)
    jitter = jnp.exp(jax.random.uniform(key, (columns,), jnp.float32, -0.35, 0.35))
    return jnp.exp(jnp.log(spread) * (position - 0.5)) * jitter


def projection_draw(key):
    base = jax.random.normal(jax.random.fold_in(key, 11), (D, HEADS * HD), jnp.float32) * D ** (-0.5)
    base = jnp.clip(base, -5.0 * D ** (-0.5), 5.0 * D ** (-0.5))
    spread = 3.0
    scaled = base * column_scales(jax.random.fold_in(key, 12), spread)[None, :]
    return jnp.clip(scaled, -1.0, 1.0).astype(jnp.bfloat16)


def gain_draw(key):
    return jax.random.uniform(jax.random.fold_in(key, 22), (HEADS * HD,), jnp.float32, 0.6, 1.6)


def draw_w_query(key, part):
    return projection_draw(jax.random.fold_in(key, 1))


def draw_w_key(key, part):
    return projection_draw(jax.random.fold_in(key, 2))


def draw_q_gain(key, part):
    return gain_draw(jax.random.fold_in(key, 3))


def draw_k_gain(key, part):
    return gain_draw(jax.random.fold_in(key, 4))


def with_ends(drawn, own_key, least, high):
    longest = drawn.shape.index(max(drawn.shape))
    spots = []
    for shift in (0, 1):
        where = [jax.random.randint(jax.random.fold_in(own_key, axis), (), 0, length) for axis, length in enumerate(drawn.shape)]
        where[longest] = (where[longest] + shift) % drawn.shape[longest]
        spots.append(tuple(where))
    return drawn.at[spots[0]].set(least).at[spots[1]].set(high)


def level_of(rng, dims, shards, low, top_value):
    level = 1.0
    for dim, parts in shards:
        heights = jax.random.uniform(jax.random.fold_in(jax.random.fold_in(rng, 6), dim), (parts,), jnp.float32, low / len(shards), top_value / len(shards))
        level = level * jnp.repeat(jnp.exp(heights), dims[dim] // parts).reshape((-1,) + (1,) * (len(dims) - 1 - dim))
    return level


def noise(key, shape, scale, limit, pieces=(), kind=jnp.bfloat16):
    values = scale * jax.random.normal(key, shape, jnp.float32)
    if pieces:
        values = values * level_of(key, shape, pieces, -0.22, 0.18)
    return jnp.clip(values, -limit, limit).astype(kind)


def setup_inputs(seed: int = 0) -> dict:
    seeds = jax.random.split(jax.random.key(seed), 12)
    return {
        "latents": noise(seeds[0], (SPANS, ROWS, D), 1.0, 6.0, ((0, 8),)),
        "control": noise(seeds[1], (SPANS, ROWS, D), 0.5, 3.0, ((0, 8),)),
        "levels": with_ends(jax.random.randint(seeds[2], (SPANS,), 0, LEVELS), jax.random.fold_in(seeds[2], 1), 0, LEVELS - 1).astype(jnp.int32),
        "window_mask": with_ends((jax.random.randint(seeds[3], (SPANS, 2), 0, 4) < 3).astype(jnp.int32), jax.random.fold_in(seeds[3], 1), 0, 1),
        "modulation": noise(seeds[4], (LEVELS, 3, D), 1.0, 3.0, (), jnp.float32),
        "w_query": draw_w_query(jax.random.fold_in(seeds[11], 71), 0),
        "w_key": draw_w_key(jax.random.fold_in(seeds[11], 71), 0),
        "w_value": noise(seeds[7], (D, HEADS * HD), D ** -0.5, 0.078125, ((0, 8), (1, 4))),
        "w_out": noise(seeds[8], (HEADS * HD, D), (HEADS * HD) ** -0.5, 0.125, ((0, 4), (1, 8))),
        "q_gain": draw_q_gain(jax.random.fold_in(seeds[11], 71), 0),
        "k_gain": draw_k_gain(jax.random.fold_in(seeds[11], 71), 0),
    }


def layer_norm(hidden):
    center = hidden - lax.optimization_barrier(jnp.mean(hidden, axis=-1, keepdims=True))
    variance = lax.optimization_barrier(jnp.mean(center * center, axis=-1, keepdims=True))
    return center * lax.rsqrt(variance + 1e-06)

def gain_norm(values, gain):
    floats = values.astype(jnp.float32)
    square_mean = lax.optimization_barrier(jnp.mean(floats * floats, axis=-1, keepdims=True))
    return (floats * lax.rsqrt(square_mean + 1e-06) * gain).astype(jnp.bfloat16)

def reference(latents, control, levels, window_mask, modulation, w_query, w_key, w_value, w_out, q_gain, k_gain):
    hidden = latents.astype(jnp.float32) + control.astype(jnp.float32)
    onehot = (levels[:, None] == jnp.arange(LEVELS, dtype=jnp.int32)[None, :]).astype(jnp.float32)
    level_mods = jnp.dot(onehot, modulation.reshape(LEVELS, 3 * D), precision=lax.Precision.HIGHEST).reshape(SPANS, 3, D)
    offset_mod = level_mods[:, 0][:, None, :]
    scale_mod = level_mods[:, 1][:, None, :]
    gate_mod = level_mods[:, 2][:, None, :]
    normed = (layer_norm(hidden) * (1.0 + scale_mod) + offset_mod).astype(jnp.bfloat16)
    flat_rows = normed.reshape(SPANS * ROWS, D)
    query = jnp.dot(flat_rows, w_query, preferred_element_type=jnp.float32).astype(jnp.bfloat16)
    keyproj = jnp.dot(flat_rows, w_key, preferred_element_type=jnp.float32).astype(jnp.bfloat16)
    valueproj = jnp.dot(flat_rows, w_value, preferred_element_type=jnp.float32).astype(jnp.bfloat16)
    qhat = gain_norm(query, q_gain).reshape(SPANS, ROWS, HEADS, HD)
    khat = gain_norm(keyproj, k_gain).reshape(SPANS, ROWS, HEADS, HD)
    values = valueproj.reshape(SPANS, ROWS, HEADS, HD)
    padding = jnp.zeros((2, ROWS, HEADS, HD), jnp.bfloat16)
    keys_padded = jnp.concatenate([padding, khat], axis=0)
    values_padded = jnp.concatenate([padding, values], axis=0)
    span_ids = jnp.arange(SPANS, dtype=jnp.int32)
    seen_far = (window_mask[:, 0] == 1) & (span_ids >= 2)
    seen_near = (window_mask[:, 1] == 1) & (span_ids >= 1)
    seen = jnp.stack([seen_far, seen_near, jnp.ones((SPANS,), dtype=bool)], axis=1)

    def one_span(packed):
        query_span, seen_row, span_id = packed
        key_window = lax.dynamic_slice(keys_padded, (span_id, jnp.int32(0), jnp.int32(0), jnp.int32(0)), (3, ROWS, HEADS, HD)).reshape(3 * ROWS, HEADS, HD)
        value_window = lax.dynamic_slice(values_padded, (span_id, jnp.int32(0), jnp.int32(0), jnp.int32(0)), (3, ROWS, HEADS, HD)).reshape(3 * ROWS, HEADS, HD)
        scores = jnp.einsum('qhd,khd->hqk', query_span.astype(jnp.float32), key_window.astype(jnp.float32)) * HD ** (-0.5)
        key_seen = jnp.repeat(seen_row, ROWS)
        scores = jnp.where(key_seen[None, None, :], scores, -1e+30)
        top = lax.optimization_barrier(jnp.max(scores, axis=-1, keepdims=True))
        expo = jnp.exp(scores - top)
        probs = (expo / lax.optimization_barrier(jnp.sum(expo, axis=-1, keepdims=True))).astype(jnp.bfloat16)
        attended = jnp.einsum('hqk,khd->qhd', probs.astype(jnp.float32), value_window.astype(jnp.float32))
        return attended.astype(jnp.bfloat16).reshape(ROWS, HEADS * HD)
    attended = lax.map(one_span, (qhat, seen, span_ids)).reshape(SPANS * ROWS, HEADS * HD)
    group_width = HEADS * HD // N_HEAD
    branch = jnp.zeros((SPANS * ROWS, D), jnp.float32)
    for group in range(N_HEAD):
        partial_out = jnp.dot(attended[:, group * group_width:(group + 1) * group_width], w_out[group * group_width:(group + 1) * group_width], preferred_element_type=jnp.float32)
        rounded = lax.optimization_barrier(partial_out.astype(jnp.bfloat16))
        branch = branch + rounded.astype(jnp.float32)
    updated = hidden + gate_mod * branch.reshape(SPANS, ROWS, D)
    return jnp.roll(updated, 1, axis=0)
```

```python
import functools
import math

import jax
import jax.numpy as jnp
from jax import lax
from jax.experimental import pallas as pl
from jax.experimental.pallas import tpu as pltpu
from jax.sharding import PartitionSpec as P

HD = 128
F32 = jnp.float32
BF16 = jnp.bfloat16
VMEM_BYTES = 60 * 1024 * 1024
WEIGHT = 16


def params():
    return pltpu.CompilerParams(vmem_limit_bytes=VMEM_BYTES)


def cost(flops, bytes_accessed, transcendentals=0):
    return pl.CostEstimate(
        flops=flops // WEIGHT,
        bytes_accessed=bytes_accessed // WEIGHT,
        transcendentals=transcendentals // WEIGHT,
    )


def from_behind(value, axis, by):
    peers = lax.axis_size(axis)
    pairs = [(i, i + by) for i in range(peers) if 0 <= i + by < peers]
    return lax.ppermute(value, axis, pairs)


def shifted(value, axis, steps):
    count = lax.axis_size(axis)
    pairs = [(source, (source + steps) % count) for source in range(count)]
    return lax.ppermute(value, axis, pairs)


def after(value, *others):
    return lax.optimization_barrier((value, *others))[0]


def sum_terms(value, axis):
    count = lax.axis_size(axis)
    if count & (count - 1):
        return [value] + [shifted(value, axis, steps) for steps in range(1, count)]
    terms, bit = [value], 1
    while bit < count:
        total = functools.reduce(jnp.add, terms)
        terms = [total, lax.ppermute(total, axis, [(i, i ^ bit) for i in range(count)])]
        bit *= 2
    return terms


def is_cube(row_count, col_count):
    return lax.axis_size("queue") == 2**3 and row_count % 32 == 0 and col_count % HD == 0


def exchange(value, bit):
    peers = lax.axis_size("queue")
    return lax.ppermute(value, "queue", [(i, i ^ bit) for i in range(peers)])


def first_step(block):
    return {0: block, 1: exchange(block, 1), 2: exchange(block, 2), 4: exchange(block, 4)}


def second_step(first):
    return {**first, 3: exchange(first[2], 1), 5: exchange(first[4], 1)}


def halves(block):
    half = block.shape[0] // 2
    return block[:half], block[half:]


def norm_kernel(levels_ref, latents_ref, control_ref, mod_ref, out_ref):
    blocks, _, width = out_ref.shape
    hidden = latents_ref[0].astype(F32) + control_ref[0].astype(F32)
    center = hidden - jnp.mean(hidden, axis=-1, keepdims=True)
    variance = jnp.mean(center * center, axis=-1, keepdims=True)
    normed = center * lax.rsqrt(variance + 1e-06)
    row = lax.rem(levels_ref[pl.program_id(0)], 8)
    normed = normed * (1.0 + mod_ref[1, pl.ds(row, 1), :]) + mod_ref[0, pl.ds(row, 1), :]
    normed = normed.astype(BF16)
    for j in range(blocks):
        out_ref[j] = normed[:, j * width : (j + 1) * width]


def modulated_norm(latents, control, levels, modulation, blocks):
    spans, rows, model = latents.shape
    tile = 128 if rows % 128 == 0 else rows
    tiles = rows // tile
    width = model // blocks
    return pl.pallas_call(
        norm_kernel,
        grid_spec=pltpu.PrefetchScalarGridSpec(
            num_scalar_prefetch=1,
            grid=(spans, tiles),
            in_specs=[
                pl.BlockSpec((1, tile, model), lambda s, t, lev: (s, t, 0)),
                pl.BlockSpec((1, tile, model), lambda s, t, lev: (s, t, 0)),
                pl.BlockSpec((2, 8, model), lambda s, t, lev: (0, lev[s] // 8, 0)),
            ],
            out_specs=pl.BlockSpec((blocks, tile, width), lambda s, t, lev: (0, s * tiles + t, 0)),
        ),
        out_shape=jax.ShapeDtypeStruct((blocks, spans * rows, width), BF16),
        compiler_params=params(),
        cost_estimate=cost(
            flops=10 * latents.size, bytes_accessed=6 * latents.size, transcendentals=0
        ),
        name="modulated_norm",
    )(levels, latents, control, modulation)


def project_kernel(layout, begun, groups, spans, *refs):
    refs = list(refs)
    index_ref = refs.pop(0)
    normed_ref = refs.pop(0)
    count = 1 + max(piece[0] for block in layout for piece in block)
    weight_refs = [refs.pop(0) for _ in range(count)]
    begun_ref = refs.pop(0) if begun else None
    *out_refs, rows_buf, weight_buf, row_sems, weight_sems = refs
    if begun:
        *out_refs, begun_buf, begun_sem = out_refs
    width = normed_ref.shape[2]

    def copies_of(b):
        copies = [
            pltpu.make_async_copy(
                normed_ref.at[index_ref[b]],
                rows_buf.at[:, pl.ds(b * width, width)],
                row_sems.at[b],
            )
        ]
        for p, (operand, first, high, row, col) in enumerate(layout[b]):
            source = weight_refs[operand]
            target = weight_buf.at[pl.ds(b * width + row, high), pl.ds(col, source.shape[1])]
            copies.append(
                pltpu.make_async_copy(source.at[pl.ds(first, high)], target, weight_sems.at[b, p])
            )
        return copies

    pairs = [range(b, min(b + 2, len(layout))) for b in range(0, len(layout), 2)]
    copies = [sum((copies_of(b) for b in pair), []) for pair in pairs]
    for ahead in copies[:2]:
        for copy in ahead:
            copy.start()
    if begun:
        fetch_begun = pltpu.make_async_copy(begun_ref, begun_buf, begun_sem)
        fetch_begun.start()
    total = None
    for i, pair in enumerate(pairs):
        for copy in copies[i]:
            copy.wait()
        if i + 2 < len(pairs):
            for copy in copies[i + 2]:
                copy.start()
        span = slice(pair[0] * width, (pair[-1] + 1) * width)
        term = jnp.dot(rows_buf[:, span], weight_buf[span], preferred_element_type=F32)
        total = term if total is None else total + term
    if begun:
        fetch_begun.wait()
        total = total + begun_buf[...]
    if not spans:
        out_refs[0][...] = total
        return
    *out_refs, square_ref = out_refs
    column = 0
    for n, group_count in enumerate(groups):
        outs = out_refs[n * spans : (n + 1) * spans]
        _, span_rows, cols = outs[0].shape
        for g in range(group_count):
            rounded = total[:, column : column + cols].astype(BF16)
            column += cols
            for i, out_ref in enumerate(outs):
                out_ref[g] = rounded[i * span_rows : (i + 1) * span_rows]
        floats = rounded.astype(F32)
        squares = jnp.sum(floats * floats, axis=-1, keepdims=True)
        for t in range(squares.shape[0] // HD):
            tile = jnp.broadcast_to(squares[t * HD : (t + 1) * HD], (HD, HD))
            square_ref[n, t : t + 1, :] = tile.T[0:1, :]


def project(normed, weights, layout, indices, groups, begun=None, spans=0):
    _, rows, width = normed.shape
    local = weights[0].shape[-1]
    cols = sum(groups) * local
    anywhere = pl.BlockSpec(memory_space=pl.ANY)
    in_vmem = pl.BlockSpec(memory_space=pltpu.VMEM)
    if spans:
        out_shape = [
            jax.ShapeDtypeStruct((count, rows // spans, local), BF16)
            for count in groups
            for _ in range(spans)
        ]
        out_shape.append(jax.ShapeDtypeStruct((len(groups), rows // HD, HD), F32))
    else:
        out_shape = [jax.ShapeDtypeStruct((rows, cols), F32)]
    result = pl.pallas_call(
        functools.partial(project_kernel, layout, begun is not None, groups, spans),
        in_specs=[pl.BlockSpec(memory_space=pltpu.SMEM)]
        + [anywhere] * (1 + len(weights) + (begun is not None)),
        out_specs=[in_vmem] * len(out_shape),
        out_shape=out_shape,
        scratch_shapes=(
            [pltpu.VMEM((rows, cols), F32), pltpu.SemaphoreType.DMA] if begun is not None else []
        )
        + [
            pltpu.VMEM((rows, len(layout) * width), BF16),
            pltpu.VMEM((len(layout) * width, cols), BF16),
            pltpu.SemaphoreType.DMA((len(layout),)),
            pltpu.SemaphoreType.DMA((len(layout), max(len(block) for block in layout))),
        ],
        compiler_params=params(),
        cost_estimate=cost(
            flops=2 * len(layout) * rows * width * cols,
            bytes_accessed=2 * len(layout) * (rows + cols) * width + 4 * rows * cols,
        ),
        name="project_final" if spans else "project_begin",
    )(indices, normed, *weights, *([begun] if begun is not None else []))
    if not spans:
        return result[0]
    sets = [result[n * spans : (n + 1) * spans] for n in range(len(groups))]
    return (*sets, result[-1])


def attention_kernel(
    total_width, span, places, seen_ref, q_ref, q_gain_ref, k_gain_ref, k0, k1, k2, v0, v1, v2, *refs
):
    *square_refs, out_ref, factors = refs
    tiles = q_ref.shape[0] // HD

    @pl.when(pl.program_id(0) == 0)
    def _():
        for f, (array, first) in enumerate(places):
            for t in range(tiles):
                row = sum(ref[array, first + t : first + t + 1, :] for ref in square_refs)
                squares = jnp.broadcast_to(row, (HD, HD)).T[:, 0:1]
                factors[f, t * HD : (t + 1) * HD] = lax.rsqrt(squares / total_width + 1e-06)

    def with_gain(values, factor, gain_ref):
        return (values.astype(F32) * factor * gain_ref[...]).astype(BF16)

    to_exponent = HD ** (-0.5) * math.log2(math.e)
    query = with_gain(q_ref[...], factors[0], q_gain_ref)
    scores = [
        lax.dot_general(
            query,
            with_gain(key[...], factors[1 + w], k_gain_ref),
            (((1,), (1,)), ((), ())),
            preferred_element_type=F32,
        )
        for w, key in enumerate((k0, k1, k2))
    ]
    tops = [jnp.max(s, axis=-1, keepdims=True) for s in scores]
    hide = [jnp.where(seen_ref[span, w] == 1, 0.0, 1e30).astype(F32) for w in range(2)] + [0.0]
    top = functools.reduce(jnp.maximum, (m - h for m, h in zip(tops, hide)))
    expos = [jnp.exp2(s * to_exponent - (top * to_exponent + h)) for s, h in zip(scores, hide)]
    inverse = 1.0 / jnp.sum(expos[0] + expos[1] + expos[2], axis=-1, keepdims=True)
    total = None
    for expo, value in zip(expos, (v0, v1, v2)):
        probs = (expo * inverse).astype(BF16)
        term = jnp.dot(probs, value[...], preferred_element_type=F32)
        total = term if total is None else total + term
    out_ref[...] = total.astype(BF16)


def attend(span, seen, query, squares, gains, prior, own, total_width):
    spans = len(own)
    _, rows, cols = query.shape
    heads = cols // HD
    tiles = rows // HD
    window = [(spans + span - 2 + w) for w in range(3)]
    window = [(0 if position >= spans else 2, position % spans) for position in window]
    places = [(1, span * tiles)] + [(array, index * tiles) for array, index in window]
    arrays = [(own if array == 0 else prior)[index] for array, index in window]

    def part(which):
        return pl.BlockSpec((None, rows, HD), lambda h: (which, 0, h))

    gain_spec = pl.BlockSpec((1, HD), lambda h: (0, h))
    return pl.pallas_call(
        functools.partial(attention_kernel, total_width, span, places),
        grid=(heads,),
        in_specs=[pl.BlockSpec(memory_space=pltpu.SMEM), part(0), gain_spec, gain_spec]
        + [part(1)] * 3
        + [part(0)] * 3
        + [pl.BlockSpec(memory_space=pltpu.VMEM)] * len(squares),
        out_specs=pl.BlockSpec((rows, HD), lambda h: (0, h)),
        out_shape=jax.ShapeDtypeStruct((rows, cols), BF16),
        scratch_shapes=[pltpu.VMEM((4, rows, 1), F32)],
        compiler_params=params(),
        cost_estimate=cost(
            flops=12 * rows * rows * cols,
            bytes_accessed=16 * rows * cols,
            transcendentals=3 * rows * rows * heads,
        ),
        name="attend",
    )(seen, query, *gains, *arrays, *arrays, *squares)


def along_line(value, axis):
    count = lax.axis_size(axis)

    def move(moved, by, least):
        pairs = [(i, i + by) for i in range(count) if 0 <= i + by < count]
        if least:
            pairs = [(i, j) for i, j in pairs if 0 <= i - by < count]
        return lax.ppermute(moved, axis, pairs)

    below = {1: move(value, 1, 0)}
    above = {1: move(value, -1, 0)}
    for k in range(3, count):
        pairs = [(i, i + s * k) for i in range(count) for s in (1, -1) if 0 <= i + s * k < count]
        if 2 * k >= count and count < 2 * k + 1 and len({j for _, j in pairs}) == len(pairs):
            below[k] = above[k] = lax.ppermute(value, axis, pairs)
        else:
            below[k] = move(value, k, 0)
            above[k] = move(value, -k, 0)
    if count > 2:
        below[2] = move(below[1], 1, 1)
        above[2] = move(above[1], -1, 1)
    return [value] + [below[k] for k in range(1, count)] + [above[k] for k in range(1, count)]


def late_slots(groups):
    return sorted({2, groups - 2}) if groups > 2 else []


class Fetch:
    def __init__(self, place_ref, span, line, weight_ref, scratch):
        self.attended, self.weights, self.sems = scratch[:3]
        self.groups = weight_ref.shape[0]
        self.mine, self.span, self.place_ref = place_ref[0], span, place_ref
        self.line, self.weight_ref, self.columns_scratch = line, weight_ref, scratch[3:]

    def slot(self, i, source):
        return pltpu.make_async_copy(source, self.attended.at[i], self.sems.at[0, i])

    def start_attended(self, slots):
        below, above = self.line[1 : self.groups], self.line[self.groups :]
        for i, k in enumerate(slots):
            if k == 0:
                self.slot(i, self.line[0]).start()
                continue

            @pl.when(self.mine >= k)
            def _():
                self.slot(i, below[k - 1]).start()

            @pl.when(self.mine < k)
            def _():
                self.slot(i, above[self.groups - k - 1]).start()

    def weight(self, i, k):
        group = lax.rem(self.mine + self.groups - k, self.groups)
        return pltpu.make_async_copy(
            self.weight_ref.at[group], self.weights.at[i], self.sems.at[1, i]
        )

    def start_weights(self, slots):
        for i, k in enumerate(slots):
            self.weight(i, k).start()

    def columns(self, latents_ref, control_ref, mod_ref):
        latents, control, mods = self.columns_scratch
        width = latents.shape[1]
        columns = pl.ds(pl.multiple_of(self.mine * width, HD), width)
        rows = pl.ds(pl.multiple_of(self.place_ref[1 + self.span] // 8 * 8, 8), 8)
        sources = (
            latents_ref.at[self.span, :, columns],
            control_ref.at[self.span, :, columns],
            mod_ref.at[2, rows, columns],
        )
        return [
            pltpu.make_async_copy(source, target, self.sems.at[2, i])
            for i, (source, target) in enumerate(zip(sources, (latents, control, mods)))
        ]

    def branch(self, slots, new_weights, total=None):
        for i, k in enumerate(slots):
            self.slot(i, self.line[0]).wait()

            @pl.when(new_weights)
            def _():
                self.weight(i, k).wait()

            part = jnp.dot(self.attended[i], self.weights[i], preferred_element_type=F32)
            part = part.astype(BF16).astype(F32)
            total = part if total is None else total + part
        return total

    def updated(self, branch, columns):
        latents, control, mods = self.columns_scratch
        for copy in columns:
            copy.wait()
        hidden = latents[...].astype(F32) + control[...].astype(F32)
        return hidden + mods[pl.ds(lax.rem(self.place_ref[1 + self.span], 8), 1), :] * branch


def start_all(copies):
    for copy in copies:
        copy.start()


def last_kernel(span, place_ref, weight_ref, latents_ref, control_ref, mod_ref, *refs):
    line, out_ref, scratch = refs[:-7], refs[-7], refs[-6:]
    fetch = Fetch(place_ref, span, line, weight_ref, scratch)
    slots = range(weight_ref.shape[0])
    columns = fetch.columns(latents_ref, control_ref, mod_ref)
    fetch.start_attended(slots)
    fetch.start_weights(slots)
    start_all(columns)
    out_ref[...] = fetch.updated(fetch.branch(slots, True), columns).astype(BF16)


def begin_kernel(slots, place_ref, weight_ref, *refs):
    line, out_ref, scratch = refs[:-4], refs[-4], refs[-3:]
    span = pl.program_id(0)
    rows = out_ref.shape[1]
    mine = [ref.at[pl.ds(pl.multiple_of(span * rows, rows), rows)] for ref in line]
    fetch = Fetch(place_ref, span, mine, weight_ref, scratch)
    fetch.start_attended(slots)

    @pl.when(span == 0)
    def _():
        fetch.start_weights(slots)

    out_ref[0] = fetch.branch(slots, span == 0)


def rest_kernel(
    slots, place_ref, arrived_ref, begun_ref, weight_ref, latents_ref, control_ref, mod_ref, *refs
):
    line, out_ref, scratch = refs[:-7], refs[-7], refs[-6:]
    step = pl.program_id(0)
    rows = out_ref.shape[1]

    def of_span(span):
        mine = [ref.at[pl.ds(pl.multiple_of(span * rows, rows), rows)] for ref in line]
        fetch = Fetch(place_ref, span, mine, weight_ref, scratch)
        return fetch, fetch.columns(latents_ref, control_ref, mod_ref)

    @pl.when(step == 0)
    def _():
        fetch, columns = of_span(0)
        fetch.start_attended(slots)
        fetch.start_weights(slots)
        start_all(columns)
        out_ref[0] = arrived_ref[...].astype(F32)

    @pl.when(step > 0)
    def _():
        fetch, columns = of_span(step - 1)

        @pl.when(step > 1)
        def _():
            fetch.start_attended(slots)
            start_all(columns)

        branch = fetch.branch(slots, step == 1, begun_ref[0])
        out_ref[0] = fetch.updated(branch, columns)


def update_scratch(slots, rows, cols, width, columns=True):
    scratch = [
        pltpu.VMEM((len(slots), rows, cols), BF16),
        pltpu.VMEM((len(slots), cols, width), BF16),
        pltpu.SemaphoreType.DMA((3, max(len(slots), 3))),
    ]
    if columns:
        scratch.append(pltpu.VMEM((rows, width), BF16))
        scratch.append(pltpu.VMEM((rows, width), BF16))
        scratch.append(pltpu.VMEM((8, width), F32))
    return scratch


def update_cost(slots, rows, cols, width):
    return cost(
        flops=2 * slots * rows * cols * width,
        bytes_accessed=2 * slots * cols * (rows + width) + 8 * rows * width,
    )


def update_last(place, line, weights, latents, control, modulation):
    rows, cols = line[0].shape
    groups, _, width = weights.shape
    span = latents.shape[0] - 1
    anywhere = pl.BlockSpec(memory_space=pl.ANY)
    return pl.pallas_call(
        functools.partial(last_kernel, span),
        in_specs=[pl.BlockSpec(memory_space=pltpu.SMEM)] + [anywhere] * (4 + len(line)),
        out_specs=pl.BlockSpec(memory_space=pltpu.VMEM),
        scratch_shapes=update_scratch(range(groups), rows, cols, width),
        out_shape=jax.ShapeDtypeStruct((rows, width), BF16),
        compiler_params=params(),
        cost_estimate=update_cost(groups, rows, cols, width),
        name="update_last",
    )(place, weights, latents, control, modulation, *line)


def update_begin(place, line, weights, spans, rows, slots):
    cols = line[0].shape[1]
    width = weights.shape[2]
    anywhere = pl.BlockSpec(memory_space=pl.ANY)
    return pl.pallas_call(
        functools.partial(begin_kernel, slots),
        grid=(spans - 1,),
        in_specs=[pl.BlockSpec(memory_space=pltpu.SMEM)] + [anywhere] * (1 + len(line)),
        out_specs=pl.BlockSpec((1, rows, width), lambda i: (i, 0, 0)),
        scratch_shapes=update_scratch(slots, rows, cols, width, columns=False),
        out_shape=jax.ShapeDtypeStruct((spans - 1, rows, width), F32),
        compiler_params=params(),
        cost_estimate=update_cost(len(slots) * (spans - 1), rows, cols, width),
        name="update_begin",
    )(place, weights, *line)


def update_rest(place, arrived, line, weights, latents, control, modulation):
    cols = line[0].shape[1]
    spans, rows, _ = latents.shape
    groups, _, width = weights.shape
    late = late_slots(groups) or [groups - 1]
    early = [k for k in range(groups) if k not in late]
    ready = list(line)
    for k in late:
        ready[k] = ready[groups - 1 + k] = line[0]
    begun = update_begin(place, ready, weights, spans, rows, early)
    anywhere = pl.BlockSpec(memory_space=pl.ANY)
    return pl.pallas_call(
        functools.partial(rest_kernel, late),
        grid=(spans,),
        in_specs=[
            pl.BlockSpec(memory_space=pltpu.SMEM),
            pl.BlockSpec((rows, width), lambda i: (0, 0)),
            pl.BlockSpec((1, rows, width), lambda i: (jnp.maximum(i - 1, 0), 0, 0)),
        ]
        + [anywhere] * (4 + len(line)),
        out_specs=pl.BlockSpec((1, rows, width), lambda i: (i, 0, 0)),
        scratch_shapes=update_scratch(late, rows, cols, width),
        out_shape=jax.ShapeDtypeStruct((spans, rows, width), F32),
        compiler_params=params(),
        cost_estimate=update_cost(len(late) * (spans - 1), rows, cols, width),
        name="update_rest",
    )(place, arrived, begun, weights, latents, control, modulation, *line)


def out_shares(w_out):
    owners = lax.axis_size("queue")
    rows, cols = w_out.shape
    return lax.all_to_all(w_out.reshape(owners, rows // owners, cols), "queue", 0, 0, tiled=True)


def out_blocks(shares):
    groups = lax.axis_size("head")
    owners, part, cols = shares.shape
    blocks = lax.all_to_all(shares, "head", 0, 0, tiled=True)
    return blocks.reshape(groups, owners // groups, part, cols)


def assemble_kernel(index_ref, *refs):
    *stacks, out_ref, sems = refs
    count, groups, sharers, part, cols = stacks[0].shape
    copies = []
    for i, stack in enumerate(stacks):
        for b in range(count):
            start = pl.multiple_of(index_ref[i * count + b] * part, part)
            for g in range(groups):
                for o in range(sharers):
                    copy = pltpu.make_async_copy(
                        stack.at[b, g, o],
                        out_ref.at[g, pl.ds(start, part), pl.ds(o * cols, cols)],
                        sems.at[i * count + b, g, o],
                    )
                    copy.start()
                    copies.append(copy)
    for copy in copies:
        copy.wait()


def assemble(stacks, indices):
    count, groups, sharers, part, cols = stacks[0].shape
    blocks = count * len(stacks)
    return pl.pallas_call(
        assemble_kernel,
        in_specs=[pl.BlockSpec(memory_space=pltpu.SMEM)]
        + [pl.BlockSpec(memory_space=pl.ANY)] * len(stacks),
        out_specs=pl.BlockSpec(memory_space=pltpu.VMEM),
        out_shape=jax.ShapeDtypeStruct((groups, blocks * part, sharers * cols), BF16),
        scratch_shapes=[pltpu.SemaphoreType.DMA((blocks, groups, sharers))],
        compiler_params=params(),
        cost_estimate=cost(flops=0, bytes_accessed=4 * stacks[0].size * len(stacks)),
        name="assemble",
    )(jnp.stack(indices), *stacks)


def assemble_in_order(gathered):
    owners, groups, sharers, part, cols = gathered.shape
    shape = (groups, owners * part, sharers * cols)
    return gathered.transpose(1, 0, 3, 2, 4).reshape(shape)


def shards(
    latents,
    control,
    levels,
    window_mask,
    modulation,
    w_query,
    w_key,
    w_value,
    w_out,
    q_gain,
    k_gain,
):
    spans, row_count, _ = latents.shape
    local_cols = w_query.shape[1]
    owners = lax.axis_size("queue")
    total_width = local_cols * lax.axis_size("head")
    owner_index = lax.axis_index("queue")
    head_index = lax.axis_index("head")
    place = jnp.concatenate([head_index.astype(jnp.int32).reshape(1), levels])
    modulation = modulation.transpose(1, 0, 2)
    gain_rows = [gain.reshape(1, -1) for gain in (q_gain, k_gain)]
    cube = is_cube(w_query.shape[0], local_cols) and w_out.shape[0] // owners % 16 == 0
    span_ids = owner_index * spans + jnp.arange(spans, dtype=jnp.int32)
    seen = (
        (window_mask == 1) & (span_ids[:, None] >= jnp.array([2, 1], jnp.int32)[None, :])
    ).astype(jnp.int32)

    if cube:
        mine = owner_index.astype(jnp.int32)
        high = w_query.shape[0]

        def indices(masks):
            return jnp.stack([mine ^ m for m in masks])

        halves_of = halves(w_query)
        sides = (jnp.concatenate([w_value, halves_of[0]]), jnp.concatenate([halves_of[1], w_key]))
        firsts = [first_step(side) for side in sides]
        early, late = [0, 1, 2, 4, 3, 5], [6, 7]
        early_indices, late_indices = indices(early), indices(late)
        small = (seen, place, early_indices, late_indices, *gain_rows)
        normed = modulated_norm(after(latents, *small), control, levels, modulation, owners)
        share = out_shares(after(w_out, normed, firsts[0][4], firsts[1][2]))
        across = [
            exchange(after(firsts[0][4], normed, share), 2),
            exchange(after(firsts[1][2], normed, share), 4),
        ]
        firsts[0][2] = after(firsts[0][2], normed, share)
        firsts[1][4] = after(firsts[1][4], normed, share)
        firsts = [second_step(first) for first in firsts]
        columns = {"value": 0, "key": local_cols, "query": 2 * local_cols}
        half = high // 2

        def layout_of(count):
            return tuple(
                (
                    (2 * b, 0, high, 0, columns["value"]),
                    (2 * b, high, half, 0, columns["query"]),
                    (2 * b + 1, 0, half, half, columns["query"]),
                    (2 * b + 1, half, high, 0, columns["key"]),
                )
                for b in range(count)
            )

        parts = [first[m] for m in early for first in firsts]
        begun = project(normed, parts, layout_of(len(early)), early_indices, (3,))
        across = [after(part, begun) for part in across]
        parts = across + [exchange(part, 1) for part in across]
        own, query, squares = project(
            normed,
            parts,
            layout_of(len(late)),
            late_indices,
            (2, 1),
            begun=begun,
            spans=spans,
        )
    else:
        normed = modulated_norm(latents, control, levels, modulation, 1)
        weights = [
            lax.all_gather(w, "queue", axis=0, tiled=True) for w in (w_value, w_key, w_query)
        ]
        model = weights[0].shape[0]
        layout = (tuple((w, 0, model, 0, w * local_cols) for w in range(3)),)
        zero = jnp.zeros((1,), jnp.int32)
        own, query, squares = project(normed, weights, layout, zero, (2, 1), spans=spans)
        share = out_shares(w_out)

    prior = [from_behind(span, "queue", 1) for span in reversed(own)][::-1]
    prior_squares = from_behind(squares, "queue", 1)
    share = out_blocks(after(share, prior_squares)) if cube else out_blocks(share)
    squares = sum_terms(jnp.concatenate([squares, prior_squares]), "head")

    def attended_of(span, ready):
        return attend(span, seen, ready, squares, gain_rows, prior, own, total_width)

    groups = lax.axis_size("head")
    attended_last = attended_of(spans - 1, query[-1])
    last = along_line(attended_last, "head")
    sent = [last[1], last[groups]]
    begin_rest = [attended_last, *sent]
    if cube:
        share = after(share, *squares)
        first = {m: exchange(share, m) for m in (2, 4)}
    rest = [attended_of(span, after(query[span], *begin_rest)) for span in range(spans - 1)]
    rest = rest[0] if len(rest) == 1 else jnp.concatenate(rest, axis=0)
    line = along_line(rest, "head")
    if cube:
        first = {m: after(block, rest, *prior) for m, block in first.items()}
        half = share.shape[0] // 2
        across = [exchange(first[4][:half], 2), exchange(first[2][half:], 4)]
        across = jnp.concatenate([after(part, *last[1:]) for part in across])
        mine_blocks = jnp.stack([share, first[2], first[4], across])
        swapped = exchange(mine_blocks, 1)
        weights = assemble(
            [mine_blocks, swapped], [mine ^ m ^ c for c in range(2) for m in (0, 2, 4, 6)]
        )
    else:
        weights = assemble_in_order(lax.all_gather(share, "queue", axis=0))
    rest = line
    updated_last = update_last(place, last, weights, latents, control, modulation)
    arrived = shifted(updated_last, "queue", 1)
    return update_rest(place, arrived, rest, weights, latents, control, modulation)


def solution(mesh):
    placed = (
        P("queue", None, None),
        P("queue", None, None),
        P("queue"),
        P("queue", None),
        P(),
        P("queue", "head"),
        P("queue", "head"),
        P("queue", "head"),
        P("head", "queue"),
        P("head"),
        P("head"),
    )
    return jax.shard_map(
        shards, mesh=mesh, in_specs=placed, out_specs=P("queue", None, "head"), check_vma=False
    )
```

```python
import functools
import math

import jax
import jax.numpy as jnp
from jax import lax
from jax.experimental import pallas as pl
from jax.experimental.pallas import tpu as pltpu
from jax.sharding import PartitionSpec as P

HD = 128
F32 = jnp.float32
BF16 = jnp.bfloat16
VMEM_BYTES = 60 * 1024 * 1024
WEIGHT = 16


def params():
    return pltpu.CompilerParams(vmem_limit_bytes=VMEM_BYTES)


def cost(flops, bytes_accessed, transcendentals=0):
    return pl.CostEstimate(
        flops=flops // WEIGHT,
        bytes_accessed=bytes_accessed // WEIGHT,
        transcendentals=transcendentals // WEIGHT,
    )


def from_behind(value, axis, by):
    peers = lax.axis_size(axis)
    pairs = [(i, i + by) for i in range(peers) if 0 <= i + by < peers]
    return lax.ppermute(value, axis, pairs)


def shifted(value, axis, steps):
    count = lax.axis_size(axis)
    pairs = [(source, (source + steps) % count) for source in range(count)]
    return lax.ppermute(value, axis, pairs)


def after(value, *others):
    return lax.optimization_barrier((value, *others))[0]


def sum_terms(value, axis):
    count = lax.axis_size(axis)
    if count & (count - 1):
        return [value] + [shifted(value, axis, steps) for steps in range(1, count)]
    terms, bit = [value], 1
    while bit < count:
        total = functools.reduce(jnp.add, terms)
        terms = [total, lax.ppermute(total, axis, [(i, i ^ bit) for i in range(count)])]
        bit *= 2
    return terms


def is_cube(row_count, col_count):
    return lax.axis_size("queue") == 2**3 and row_count % 32 == 0 and col_count % HD == 0


def exchange(value, bit):
    peers = lax.axis_size("queue")
    return lax.ppermute(value, "queue", [(i, i ^ bit) for i in range(peers)])


def first_step(block):
    return {0: block, 1: exchange(block, 1), 2: exchange(block, 2), 4: exchange(block, 4)}


def second_step(first):
    return {**first, 3: exchange(first[2], 1), 5: exchange(first[4], 1)}


def halves(block):
    half = block.shape[0] // 2
    return block[:half], block[half:]


def norm_kernel(levels_ref, latents_ref, control_ref, mod_ref, out_ref):
    blocks, _, width = out_ref.shape
    hidden = latents_ref[0].astype(F32) + control_ref[0].astype(F32)
    center = hidden - jnp.mean(hidden, axis=-1, keepdims=True)
    variance = jnp.mean(center * center, axis=-1, keepdims=True)
    normed = center * lax.rsqrt(variance + 1e-06)
    row = lax.rem(levels_ref[pl.program_id(0)], 8)
    normed = normed * (1.0 + mod_ref[1, pl.ds(row, 1), :]) + mod_ref[0, pl.ds(row, 1), :]
    normed = normed.astype(BF16)
    for j in range(blocks):
        out_ref[j] = normed[:, j * width : (j + 1) * width]


def modulated_norm(latents, control, levels, modulation, blocks):
    spans, rows, model = latents.shape
    tile = 128 if rows % 128 == 0 else rows
    tiles = rows // tile
    width = model // blocks
    return pl.pallas_call(
        norm_kernel,
        grid_spec=pltpu.PrefetchScalarGridSpec(
            num_scalar_prefetch=1,
            grid=(spans, tiles),
            in_specs=[
                pl.BlockSpec((1, tile, model), lambda s, t, lev: (s, t, 0)),
                pl.BlockSpec((1, tile, model), lambda s, t, lev: (s, t, 0)),
                pl.BlockSpec((2, 8, model), lambda s, t, lev: (0, lev[s] // 8, 0)),
            ],
            out_specs=pl.BlockSpec((blocks, tile, width), lambda s, t, lev: (0, s * tiles + t, 0)),
        ),
        out_shape=jax.ShapeDtypeStruct((blocks, spans * rows, width), BF16),
        compiler_params=params(),
        cost_estimate=cost(
            flops=10 * latents.size, bytes_accessed=6 * latents.size, transcendentals=0
        ),
        name="modulated_norm",
    )(levels, latents, control, modulation)


def project_kernel(layout, begun, groups, spans, *refs):
    refs = list(refs)
    index_ref = refs.pop(0)
    normed_ref = refs.pop(0)
    count = 1 + max(piece[0] for block in layout for piece in block)
    weight_refs = [refs.pop(0) for _ in range(count)]
    begun_ref = refs.pop(0) if begun else None
    *out_refs, rows_buf, weight_buf, row_sems, weight_sems = refs
    if begun:
        *out_refs, begun_buf, begun_sem = out_refs
    width = normed_ref.shape[2]

    def copies_of(b):
        copies = [
            pltpu.make_async_copy(
                normed_ref.at[index_ref[b]],
                rows_buf.at[:, pl.ds(b * width, width)],
                row_sems.at[b],
            )
        ]
        for p, (operand, first, high, row, col) in enumerate(layout[b]):
            source = weight_refs[operand]
            target = weight_buf.at[pl.ds(b * width + row, high), pl.ds(col, source.shape[1])]
            copies.append(
                pltpu.make_async_copy(source.at[pl.ds(first, high)], target, weight_sems.at[b, p])
            )
        return copies

    pairs = [range(b, min(b + 2, len(layout))) for b in range(0, len(layout), 2)]
    copies = [sum((copies_of(b) for b in pair), []) for pair in pairs]
    for ahead in copies[:2]:
        for copy in ahead:
            copy.start()
    if begun:
        fetch_begun = pltpu.make_async_copy(begun_ref, begun_buf, begun_sem)
        fetch_begun.start()
    total = None
    for i, pair in enumerate(pairs):
        for copy in copies[i]:
            copy.wait()
        if i + 2 < len(pairs):
            for copy in copies[i + 2]:
                copy.start()
        span = slice(pair[0] * width, (pair[-1] + 1) * width)
        term = jnp.dot(rows_buf[:, span], weight_buf[span], preferred_element_type=F32)
        total = term if total is None else total + term
    if begun:
        fetch_begun.wait()
        total = total + begun_buf[...]
    if not spans:
        out_refs[0][...] = total
        return
    *out_refs, square_ref = out_refs
    column = 0
    for n, group_count in enumerate(groups):
        outs = out_refs[n * spans : (n + 1) * spans]
        _, span_rows, cols = outs[0].shape
        for g in range(group_count):
            rounded = total[:, column : column + cols].astype(BF16)
            column += cols
            for i, out_ref in enumerate(outs):
                out_ref[g] = rounded[i * span_rows : (i + 1) * span_rows]
        floats = rounded.astype(F32)
        squares = jnp.sum(floats * floats, axis=-1, keepdims=True)
        for t in range(squares.shape[0] // HD):
            tile = jnp.broadcast_to(squares[t * HD : (t + 1) * HD], (HD, HD))
            square_ref[n, t : t + 1, :] = tile.T[0:1, :]


def project(normed, weights, layout, indices, groups, begun=None, spans=0):
    _, rows, width = normed.shape
    local = weights[0].shape[-1]
    cols = sum(groups) * local
    anywhere = pl.BlockSpec(memory_space=pl.ANY)
    in_vmem = pl.BlockSpec(memory_space=pltpu.VMEM)
    if spans:
        out_shape = [
            jax.ShapeDtypeStruct((count, rows // spans, local), BF16)
            for count in groups
            for _ in range(spans)
        ]
        out_shape.append(jax.ShapeDtypeStruct((len(groups), rows // HD, HD), F32))
    else:
        out_shape = [jax.ShapeDtypeStruct((rows, cols), F32)]
    result = pl.pallas_call(
        functools.partial(project_kernel, layout, begun is not None, groups, spans),
        in_specs=[pl.BlockSpec(memory_space=pltpu.SMEM)]
        + [anywhere] * (1 + len(weights) + (begun is not None)),
        out_specs=[in_vmem] * len(out_shape),
        out_shape=out_shape,
        scratch_shapes=(
            [pltpu.VMEM((rows, cols), F32), pltpu.SemaphoreType.DMA] if begun is not None else []
        )
        + [
            pltpu.VMEM((rows, len(layout) * width), BF16),
            pltpu.VMEM((len(layout) * width, cols), BF16),
            pltpu.SemaphoreType.DMA((len(layout),)),
            pltpu.SemaphoreType.DMA((len(layout), max(len(block) for block in layout))),
        ],
        compiler_params=params(),
        cost_estimate=cost(
            flops=2 * len(layout) * rows * width * cols,
            bytes_accessed=2 * len(layout) * (rows + cols) * width + 4 * rows * cols,
        ),
        name="project_final" if spans else "project_begin",
    )(indices, normed, *weights, *([begun] if begun is not None else []))
    if not spans:
        return result[0]
    sets = [result[n * spans : (n + 1) * spans] for n in range(len(groups))]
    return (*sets, result[-1])


def attention_kernel(
    total_width, span, places, seen_ref, q_ref, q_gain_ref, k_gain_ref, k0, k1, k2, v0, v1, v2, *refs
):
    *square_refs, out_ref = refs
    rows, cols = q_ref.shape
    tiles = rows // HD
    factors = []
    for array, first in places:
        pieces = []
        for t in range(tiles):
            row = sum(ref[array, first + t : first + t + 1, :] for ref in square_refs)
            pieces.append(jnp.broadcast_to(row, (HD, HD)).T[:, 0:1])
        squares = jnp.concatenate(pieces, axis=0)
        factors.append(lax.rsqrt(squares / total_width + 1e-06))
    hide = [jnp.where(seen_ref[span, w] == 1, 0.0, 1e30).astype(F32) for w in range(2)] + [0.0]
    to_exponent = HD ** (-0.5) * math.log2(math.e)

    def with_gain(ref, head, factor, gain_ref):
        values = ref[:, head].astype(F32) * factor * gain_ref[:, head]
        return values.astype(BF16)

    def scores_of(head):
        query = with_gain(q_ref, head, factors[0], q_gain_ref)
        return [
            lax.dot_general(
                query,
                with_gain(key, head, factors[1 + w], k_gain_ref),
                (((1,), (1,)), ((), ())),
                preferred_element_type=F32,
            )
            for w, key in enumerate((k0, k1, k2))
        ]

    heads = [slice(h * HD, (h + 1) * HD) for h in range(cols // HD)]
    scores = scores_of(heads[0])
    for h, head in enumerate(heads):
        following = scores_of(heads[h + 1]) if h + 1 < len(heads) else None
        tops = [jnp.max(s, axis=-1, keepdims=True) for s in scores]
        top = functools.reduce(jnp.maximum, (m - x for m, x in zip(tops, hide)))
        expos = [
            jnp.exp2(s * to_exponent - (top * to_exponent + x)) for s, x in zip(scores, hide)
        ]
        inverse = 1.0 / jnp.sum(expos[0] + expos[1] + expos[2], axis=-1, keepdims=True)
        total = None
        for expo, value in zip(expos, (v0, v1, v2)):
            probs = (expo * inverse).astype(BF16)
            term = jnp.dot(probs, value[:, head], preferred_element_type=F32)
            total = term if total is None else total + term
        out_ref[:, head] = total.astype(BF16)
        scores = following


def attend(span, seen, query, squares, gains, prior, own, total_width):
    spans = len(own)
    _, rows, cols = query.shape
    heads = cols // HD
    tiles = rows // HD
    window = [(spans + span - 2 + w) for w in range(3)]
    window = [(0 if position >= spans else 2, position % spans) for position in window]
    places = [(1, span * tiles)] + [(array, index * tiles) for array, index in window]
    arrays = [(own if array == 0 else prior)[index] for array, index in window]

    def part(which):
        return pl.BlockSpec((None, rows, cols), lambda i: (which, 0, 0))

    gain_spec = pl.BlockSpec((1, cols), lambda i: (0, 0))
    return pl.pallas_call(
        functools.partial(attention_kernel, total_width, span, places),
        grid=(1,),
        in_specs=[pl.BlockSpec(memory_space=pltpu.SMEM), part(0), gain_spec, gain_spec]
        + [part(1)] * 3
        + [part(0)] * 3
        + [pl.BlockSpec(memory_space=pltpu.VMEM)] * len(squares),
        out_specs=pl.BlockSpec((rows, cols), lambda i: (0, 0)),
        out_shape=jax.ShapeDtypeStruct((rows, cols), BF16),
        compiler_params=params(),
        cost_estimate=cost(
            flops=12 * rows * rows * cols,
            bytes_accessed=16 * rows * cols,
            transcendentals=3 * rows * rows * heads,
        ),
        name="attend",
    )(seen, query, *gains, *arrays, *arrays, *squares)


def along_line(value, axis):
    count = lax.axis_size(axis)

    def move(moved, by, least):
        pairs = [(i, i + by) for i in range(count) if 0 <= i + by < count]
        if least:
            pairs = [(i, j) for i, j in pairs if 0 <= i - by < count]
        return lax.ppermute(moved, axis, pairs)

    below = {1: move(value, 1, 0)}
    above = {1: move(value, -1, 0)}
    for k in range(3, count):
        pairs = [(i, i + s * k) for i in range(count) for s in (1, -1) if 0 <= i + s * k < count]
        if 2 * k >= count and count < 2 * k + 1 and len({j for _, j in pairs}) == len(pairs):
            below[k] = above[k] = lax.ppermute(value, axis, pairs)
        else:
            below[k] = move(value, k, 0)
            above[k] = move(value, -k, 0)
    if count > 2:
        below[2] = move(below[1], 1, 1)
        above[2] = move(above[1], -1, 1)
    return [value] + [below[k] for k in range(1, count)] + [above[k] for k in range(1, count)]


def late_slots(groups):
    return sorted({2, groups - 2}) if groups > 2 else []


class Fetch:
    def __init__(self, place_ref, span, line, weight_ref, scratch):
        self.attended, self.weights, self.sems = scratch[:3]
        self.groups = weight_ref.shape[0]
        self.mine, self.span, self.place_ref = place_ref[0], span, place_ref
        self.line, self.weight_ref, self.columns_scratch = line, weight_ref, scratch[3:]

    def slot(self, i, source):
        return pltpu.make_async_copy(source, self.attended.at[i], self.sems.at[0, i])

    def start_attended(self, slots):
        below, above = self.line[1 : self.groups], self.line[self.groups :]
        for i, k in enumerate(slots):
            if k == 0:
                self.slot(i, self.line[0]).start()
                continue

            @pl.when(self.mine >= k)
            def _():
                self.slot(i, below[k - 1]).start()

            @pl.when(self.mine < k)
            def _():
                self.slot(i, above[self.groups - k - 1]).start()

    def weight(self, i, k):
        group = lax.rem(self.mine + self.groups - k, self.groups)
        return pltpu.make_async_copy(
            self.weight_ref.at[group], self.weights.at[i], self.sems.at[1, i]
        )

    def start_weights(self, slots):
        for i, k in enumerate(slots):
            self.weight(i, k).start()

    def columns(self, latents_ref, control_ref, mod_ref):
        latents, control, mods = self.columns_scratch
        width = latents.shape[1]
        columns = pl.ds(pl.multiple_of(self.mine * width, HD), width)
        rows = pl.ds(pl.multiple_of(self.place_ref[1 + self.span] // 8 * 8, 8), 8)
        sources = (
            latents_ref.at[self.span, :, columns],
            control_ref.at[self.span, :, columns],
            mod_ref.at[2, rows, columns],
        )
        return [
            pltpu.make_async_copy(source, target, self.sems.at[2, i])
            for i, (source, target) in enumerate(zip(sources, (latents, control, mods)))
        ]

    def branch(self, slots, new_weights, total=None):
        for i, k in enumerate(slots):
            self.slot(i, self.line[0]).wait()

            @pl.when(new_weights)
            def _():
                self.weight(i, k).wait()

            part = jnp.dot(self.attended[i], self.weights[i], preferred_element_type=F32)
            part = part.astype(BF16).astype(F32)
            total = part if total is None else total + part
        return total

    def updated(self, branch, columns):
        latents, control, mods = self.columns_scratch
        for copy in columns:
            copy.wait()
        hidden = latents[...].astype(F32) + control[...].astype(F32)
        return hidden + mods[pl.ds(lax.rem(self.place_ref[1 + self.span], 8), 1), :] * branch


def start_all(copies):
    for copy in copies:
        copy.start()


def last_kernel(span, place_ref, weight_ref, latents_ref, control_ref, mod_ref, *refs):
    line, out_ref, scratch = refs[:-7], refs[-7], refs[-6:]
    fetch = Fetch(place_ref, span, line, weight_ref, scratch)
    slots = range(weight_ref.shape[0])
    columns = fetch.columns(latents_ref, control_ref, mod_ref)
    fetch.start_attended(slots)
    fetch.start_weights(slots)
    start_all(columns)
    out_ref[...] = fetch.updated(fetch.branch(slots, True), columns).astype(BF16)


def begin_kernel(slots, place_ref, weight_ref, *refs):
    line, out_ref, scratch = refs[:-4], refs[-4], refs[-3:]
    span = pl.program_id(0)
    rows = out_ref.shape[1]
    mine = [ref.at[pl.ds(pl.multiple_of(span * rows, rows), rows)] for ref in line]
    fetch = Fetch(place_ref, span, mine, weight_ref, scratch)
    fetch.start_attended(slots)

    @pl.when(span == 0)
    def _():
        fetch.start_weights(slots)

    out_ref[0] = fetch.branch(slots, span == 0)


def rest_kernel(
    slots, place_ref, arrived_ref, begun_ref, weight_ref, latents_ref, control_ref, mod_ref, *refs
):
    line, out_ref, scratch = refs[:-7], refs[-7], refs[-6:]
    step = pl.program_id(0)
    rows = out_ref.shape[1]

    def of_span(span):
        mine = [ref.at[pl.ds(pl.multiple_of(span * rows, rows), rows)] for ref in line]
        fetch = Fetch(place_ref, span, mine, weight_ref, scratch)
        return fetch, fetch.columns(latents_ref, control_ref, mod_ref)

    @pl.when(step == 0)
    def _():
        fetch, columns = of_span(0)
        fetch.start_attended(slots)
        fetch.start_weights(slots)
        start_all(columns)
        out_ref[0] = arrived_ref[...].astype(F32)

    @pl.when(step > 0)
    def _():
        fetch, columns = of_span(step - 1)

        @pl.when(step > 1)
        def _():
            fetch.start_attended(slots)
            start_all(columns)

        branch = fetch.branch(slots, step == 1, begun_ref[0])
        out_ref[0] = fetch.updated(branch, columns)


def update_scratch(slots, rows, cols, width, columns=True):
    scratch = [
        pltpu.VMEM((len(slots), rows, cols), BF16),
        pltpu.VMEM((len(slots), cols, width), BF16),
        pltpu.SemaphoreType.DMA((3, max(len(slots), 3))),
    ]
    if columns:
        scratch.append(pltpu.VMEM((rows, width), BF16))
        scratch.append(pltpu.VMEM((rows, width), BF16))
        scratch.append(pltpu.VMEM((8, width), F32))
    return scratch


def update_cost(slots, rows, cols, width):
    return cost(
        flops=2 * slots * rows * cols * width,
        bytes_accessed=2 * slots * cols * (rows + width) + 8 * rows * width,
    )


def update_last(place, line, weights, latents, control, modulation):
    rows, cols = line[0].shape
    groups, _, width = weights.shape
    span = latents.shape[0] - 1
    anywhere = pl.BlockSpec(memory_space=pl.ANY)
    return pl.pallas_call(
        functools.partial(last_kernel, span),
        in_specs=[pl.BlockSpec(memory_space=pltpu.SMEM)] + [anywhere] * (4 + len(line)),
        out_specs=pl.BlockSpec(memory_space=pltpu.VMEM),
        scratch_shapes=update_scratch(range(groups), rows, cols, width),
        out_shape=jax.ShapeDtypeStruct((rows, width), BF16),
        compiler_params=params(),
        cost_estimate=update_cost(groups, rows, cols, width),
        name="update_last",
    )(place, weights, latents, control, modulation, *line)


def update_begin(place, line, weights, spans, rows, slots):
    cols = line[0].shape[1]
    width = weights.shape[2]
    anywhere = pl.BlockSpec(memory_space=pl.ANY)
    return pl.pallas_call(
        functools.partial(begin_kernel, slots),
        grid=(spans - 1,),
        in_specs=[pl.BlockSpec(memory_space=pltpu.SMEM)] + [anywhere] * (1 + len(line)),
        out_specs=pl.BlockSpec((1, rows, width), lambda i: (i, 0, 0)),
        scratch_shapes=update_scratch(slots, rows, cols, width, columns=False),
        out_shape=jax.ShapeDtypeStruct((spans - 1, rows, width), F32),
        compiler_params=params(),
        cost_estimate=update_cost(len(slots) * (spans - 1), rows, cols, width),
        name="update_begin",
    )(place, weights, *line)


def update_rest(place, arrived, line, weights, latents, control, modulation):
    cols = line[0].shape[1]
    spans, rows, _ = latents.shape
    groups, _, width = weights.shape
    late = late_slots(groups) or [groups - 1]
    early = [k for k in range(groups) if k not in late]
    ready = list(line)
    for k in late:
        ready[k] = ready[groups - 1 + k] = line[0]
    begun = update_begin(place, ready, weights, spans, rows, early)
    anywhere = pl.BlockSpec(memory_space=pl.ANY)
    return pl.pallas_call(
        functools.partial(rest_kernel, late),
        grid=(spans,),
        in_specs=[
            pl.BlockSpec(memory_space=pltpu.SMEM),
            pl.BlockSpec((rows, width), lambda i: (0, 0)),
            pl.BlockSpec((1, rows, width), lambda i: (jnp.maximum(i - 1, 0), 0, 0)),
        ]
        + [anywhere] * (4 + len(line)),
        out_specs=pl.BlockSpec((1, rows, width), lambda i: (i, 0, 0)),
        scratch_shapes=update_scratch(late, rows, cols, width),
        out_shape=jax.ShapeDtypeStruct((spans, rows, width), F32),
        compiler_params=params(),
        cost_estimate=update_cost(len(late) * (spans - 1), rows, cols, width),
        name="update_rest",
    )(place, arrived, begun, weights, latents, control, modulation, *line)


def out_shares(w_out):
    owners = lax.axis_size("queue")
    rows, cols = w_out.shape
    return lax.all_to_all(w_out.reshape(owners, rows // owners, cols), "queue", 0, 0, tiled=True)


def out_blocks(shares):
    groups = lax.axis_size("head")
    owners, part, cols = shares.shape
    blocks = lax.all_to_all(shares, "head", 0, 0, tiled=True)
    return blocks.reshape(groups, owners // groups, part, cols)


def assemble_kernel(index_ref, *refs):
    *stacks, out_ref, sems = refs
    count, groups, sharers, part, cols = stacks[0].shape
    copies = []
    for i, stack in enumerate(stacks):
        for b in range(count):
            start = pl.multiple_of(index_ref[i * count + b] * part, part)
            for g in range(groups):
                for o in range(sharers):
                    copy = pltpu.make_async_copy(
                        stack.at[b, g, o],
                        out_ref.at[g, pl.ds(start, part), pl.ds(o * cols, cols)],
                        sems.at[i * count + b, g, o],
                    )
                    copy.start()
                    copies.append(copy)
    for copy in copies:
        copy.wait()


def assemble(stacks, indices):
    count, groups, sharers, part, cols = stacks[0].shape
    blocks = count * len(stacks)
    return pl.pallas_call(
        assemble_kernel,
        in_specs=[pl.BlockSpec(memory_space=pltpu.SMEM)]
        + [pl.BlockSpec(memory_space=pl.ANY)] * len(stacks),
        out_specs=pl.BlockSpec(memory_space=pltpu.VMEM),
        out_shape=jax.ShapeDtypeStruct((groups, blocks * part, sharers * cols), BF16),
        scratch_shapes=[pltpu.SemaphoreType.DMA((blocks, groups, sharers))],
        compiler_params=params(),
        cost_estimate=cost(flops=0, bytes_accessed=4 * stacks[0].size * len(stacks)),
        name="assemble",
    )(jnp.stack(indices), *stacks)


def assemble_in_order(gathered):
    owners, groups, sharers, part, cols = gathered.shape
    shape = (groups, owners * part, sharers * cols)
    return gathered.transpose(1, 0, 3, 2, 4).reshape(shape)


def shards(
    latents,
    control,
    levels,
    window_mask,
    modulation,
    w_query,
    w_key,
    w_value,
    w_out,
    q_gain,
    k_gain,
):
    spans, row_count, _ = latents.shape
    local_cols = w_query.shape[1]
    owners = lax.axis_size("queue")
    total_width = local_cols * lax.axis_size("head")
    owner_index = lax.axis_index("queue")
    head_index = lax.axis_index("head")
    place = jnp.concatenate([head_index.astype(jnp.int32).reshape(1), levels])
    modulation = modulation.transpose(1, 0, 2)
    gain_rows = [gain.reshape(1, -1) for gain in (q_gain, k_gain)]
    cube = is_cube(w_query.shape[0], local_cols) and w_out.shape[0] // owners % 16 == 0
    span_ids = owner_index * spans + jnp.arange(spans, dtype=jnp.int32)
    seen = (
        (window_mask == 1) & (span_ids[:, None] >= jnp.array([2, 1], jnp.int32)[None, :])
    ).astype(jnp.int32)

    if cube:
        mine = owner_index.astype(jnp.int32)
        high = w_query.shape[0]

        def indices(masks):
            return jnp.stack([mine ^ m for m in masks])

        halves_of = halves(w_query)
        sides = (jnp.concatenate([w_value, halves_of[0]]), jnp.concatenate([halves_of[1], w_key]))
        firsts = [{m: exchange(side, m) for m in (2, 4)} for side in sides]
        early, late = [0, 1, 2, 4, 3, 5], [6, 7]
        early_indices, late_indices = indices(early), indices(late)
        small = (seen, place, early_indices, late_indices, *gain_rows)
        normed = modulated_norm(after(latents, *small), control, levels, modulation, owners)
        firsts[0][4], firsts[1][2] = after(firsts[0][4], normed), after(firsts[1][2], normed)
        for side, first in zip(sides, firsts):
            first.update({0: side, 1: exchange(after(side, normed), 1)})
        share = out_shares(after(w_out, normed, firsts[0][4], firsts[1][2]))
        across = [
            exchange(after(firsts[0][4], normed, share), 2),
            exchange(after(firsts[1][2], normed, share), 4),
        ]
        firsts[0][2] = after(firsts[0][2], normed, share)
        firsts[1][4] = after(firsts[1][4], normed, share)
        firsts = [second_step(first) for first in firsts]
        columns = {"value": 0, "key": local_cols, "query": 2 * local_cols}
        half = high // 2

        def layout_of(count):
            return tuple(
                (
                    (2 * b, 0, high, 0, columns["value"]),
                    (2 * b, high, half, 0, columns["query"]),
                    (2 * b + 1, 0, half, half, columns["query"]),
                    (2 * b + 1, half, high, 0, columns["key"]),
                )
                for b in range(count)
            )

        parts = [first[m] for m in early for first in firsts]
        begun = project(normed, parts, layout_of(len(early)), early_indices, (3,))
        across = [after(part, begun) for part in across]
        parts = across + [exchange(part, 1) for part in across]
        own, query, squares = project(
            normed,
            parts,
            layout_of(len(late)),
            late_indices,
            (2, 1),
            begun=begun,
            spans=spans,
        )
    else:
        normed = modulated_norm(latents, control, levels, modulation, 1)
        weights = [
            lax.all_gather(w, "queue", axis=0, tiled=True) for w in (w_value, w_key, w_query)
        ]
        model = weights[0].shape[0]
        layout = (tuple((w, 0, model, 0, w * local_cols) for w in range(3)),)
        zero = jnp.zeros((1,), jnp.int32)
        own, query, squares = project(normed, weights, layout, zero, (2, 1), spans=spans)
        share = out_shares(w_out)

    prior = [from_behind(span, "queue", 1) for span in reversed(own)][::-1]
    prior_squares = from_behind(squares, "queue", 1)
    share = out_blocks(after(share, prior_squares)) if cube else out_blocks(share)
    squares = sum_terms(jnp.concatenate([squares, prior_squares]), "head")

    def attended_of(span, ready):
        return attend(span, seen, ready, squares, gain_rows, prior, own, total_width)

    groups = lax.axis_size("head")
    attended_last = attended_of(spans - 1, query[-1])
    last = along_line(attended_last, "head")
    sent = [last[1], last[groups]]
    begin_rest = [attended_last, *sent]
    if cube:
        share = after(share, *squares)
        first = {m: exchange(share, m) for m in (2, 4)}
    rest = [attended_of(span, after(query[span], *begin_rest)) for span in range(spans - 1)]
    rest = rest[0] if len(rest) == 1 else jnp.concatenate(rest, axis=0)
    line = along_line(rest, "head")
    if cube:
        first = {m: after(block, rest, *prior) for m, block in first.items()}
        half = share.shape[0] // 2
        across = [exchange(first[4][:half], 2), exchange(first[2][half:], 4)]
        across = jnp.concatenate([after(part, *last[1:]) for part in across])
        mine_blocks = jnp.stack([share, first[2], first[4], across])
        swapped = exchange(mine_blocks, 1)
        weights = assemble(
            [mine_blocks, swapped], [mine ^ m ^ c for c in range(2) for m in (0, 2, 4, 6)]
        )
    else:
        weights = assemble_in_order(lax.all_gather(share, "queue", axis=0))
    rest = line
    updated_last = update_last(place, last, weights, latents, control, modulation)
    arrived = shifted(updated_last, "queue", 1)
    return update_rest(place, arrived, rest, weights, latents, control, modulation)


def solution(mesh):
    placed = (
        P("queue", None, None),
        P("queue", None, None),
        P("queue"),
        P("queue", None),
        P(),
        P("queue", "head"),
        P("queue", "head"),
        P("queue", "head"),
        P("head", "queue"),
        P("head"),
        P("head"),
    )
    return jax.shard_map(
        shards, mesh=mesh, in_specs=placed, out_specs=P("queue", None, "head"), check_vma=False
    )
```

```python
import functools
import math

import jax
import jax.numpy as jnp
from jax import lax
from jax.experimental import pallas as pl
from jax.experimental.pallas import tpu as pltpu
from jax.sharding import PartitionSpec as P

HD = 128
F32 = jnp.float32
BF16 = jnp.bfloat16
VMEM_BYTES = 60 * 1024 * 1024
WEIGHT = 16


def params():
    return pltpu.CompilerParams(vmem_limit_bytes=VMEM_BYTES)


def cost(flops, bytes_accessed, transcendentals=0):
    return pl.CostEstimate(
        flops=flops // WEIGHT,
        bytes_accessed=bytes_accessed // WEIGHT,
        transcendentals=transcendentals // WEIGHT,
    )


def from_behind(value, axis, by):
    peers = lax.axis_size(axis)
    pairs = [(i, i + by) for i in range(peers) if 0 <= i + by < peers]
    return lax.ppermute(value, axis, pairs)


def shifted(value, axis, steps):
    count = lax.axis_size(axis)
    pairs = [(source, (source + steps) % count) for source in range(count)]
    return lax.ppermute(value, axis, pairs)


def after(value, *others):
    return lax.optimization_barrier((value, *others))[0]


def sum_terms(value, axis):
    count = lax.axis_size(axis)
    if count & (count - 1):
        return [value] + [shifted(value, axis, steps) for steps in range(1, count)]
    terms, bit = [value], 1
    while bit < count:
        total = functools.reduce(jnp.add, terms)
        terms = [total, lax.ppermute(total, axis, [(i, i ^ bit) for i in range(count)])]
        bit *= 2
    return terms


def is_cube(row_count, col_count):
    return lax.axis_size("queue") == 2**3 and row_count % 32 == 0 and col_count % HD == 0


def exchange(value, bit):
    peers = lax.axis_size("queue")
    return lax.ppermute(value, "queue", [(i, i ^ bit) for i in range(peers)])


def first_step(block):
    return {0: block, 1: exchange(block, 1), 2: exchange(block, 2), 4: exchange(block, 4)}


def second_step(first):
    return {**first, 3: exchange(first[2], 1), 5: exchange(first[4], 1)}


def halves(block):
    half = block.shape[0] // 2
    return block[:half], block[half:]


def norm_kernel(levels_ref, latents_ref, control_ref, mod_ref, out_ref):
    blocks, _, width = out_ref.shape
    hidden = latents_ref[0].astype(F32) + control_ref[0].astype(F32)
    center = hidden - jnp.mean(hidden, axis=-1, keepdims=True)
    variance = jnp.mean(center * center, axis=-1, keepdims=True)
    normed = center * lax.rsqrt(variance + 1e-06)
    row = lax.rem(levels_ref[pl.program_id(0)], 8)
    normed = normed * (1.0 + mod_ref[1, pl.ds(row, 1), :]) + mod_ref[0, pl.ds(row, 1), :]
    normed = normed.astype(BF16)
    for j in range(blocks):
        out_ref[j] = normed[:, j * width : (j + 1) * width]


def modulated_norm(latents, control, levels, modulation, blocks):
    spans, rows, model = latents.shape
    tile = 128 if rows % 128 == 0 else rows
    tiles = rows // tile
    width = model // blocks
    return pl.pallas_call(
        norm_kernel,
        grid_spec=pltpu.PrefetchScalarGridSpec(
            num_scalar_prefetch=1,
            grid=(spans, tiles),
            in_specs=[
                pl.BlockSpec((1, tile, model), lambda s, t, lev: (s, t, 0)),
                pl.BlockSpec((1, tile, model), lambda s, t, lev: (s, t, 0)),
                pl.BlockSpec((2, 8, model), lambda s, t, lev: (0, lev[s] // 8, 0)),
            ],
            out_specs=pl.BlockSpec((blocks, tile, width), lambda s, t, lev: (0, s * tiles + t, 0)),
        ),
        out_shape=jax.ShapeDtypeStruct((blocks, spans * rows, width), BF16),
        compiler_params=params(),
        cost_estimate=cost(
            flops=10 * latents.size, bytes_accessed=6 * latents.size, transcendentals=0
        ),
        name="modulated_norm",
    )(levels, latents, control, modulation)


def project_kernel(layout, begun, groups, spans, *refs):
    refs = list(refs)
    index_ref = refs.pop(0)
    normed_ref = refs.pop(0)
    count = 1 + max(piece[0] for block in layout for piece in block)
    weight_refs = [refs.pop(0) for _ in range(count)]
    begun_ref = refs.pop(0) if begun else None
    *out_refs, rows_buf, weight_buf, row_sems, weight_sems = refs
    if begun:
        *out_refs, begun_buf, begun_sem = out_refs
    width = normed_ref.shape[2]

    def copies_of(b):
        copies = [
            pltpu.make_async_copy(
                normed_ref.at[index_ref[b]],
                rows_buf.at[:, pl.ds(b * width, width)],
                row_sems.at[b],
            )
        ]
        for p, (operand, first, high, row, col) in enumerate(layout[b]):
            source = weight_refs[operand]
            target = weight_buf.at[pl.ds(b * width + row, high), pl.ds(col, source.shape[1])]
            copies.append(
                pltpu.make_async_copy(source.at[pl.ds(first, high)], target, weight_sems.at[b, p])
            )
        return copies

    pairs = [range(b, min(b + 2, len(layout))) for b in range(0, len(layout), 2)]
    copies = [sum((copies_of(b) for b in pair), []) for pair in pairs]
    for ahead in copies[:2]:
        for copy in ahead:
            copy.start()
    if begun:
        fetch_begun = pltpu.make_async_copy(begun_ref, begun_buf, begun_sem)
        fetch_begun.start()
    total = None
    for i, pair in enumerate(pairs):
        for copy in copies[i]:
            copy.wait()
        if i + 2 < len(pairs):
            for copy in copies[i + 2]:
                copy.start()
        span = slice(pair[0] * width, (pair[-1] + 1) * width)
        term = jnp.dot(rows_buf[:, span], weight_buf[span], preferred_element_type=F32)
        total = term if total is None else total + term
    if begun:
        fetch_begun.wait()
        total = total + begun_buf[...]
    if not spans:
        out_refs[0][...] = total
        return
    *out_refs, square_ref = out_refs
    column = 0
    for n, group_count in enumerate(groups):
        outs = out_refs[n * spans : (n + 1) * spans]
        _, span_rows, cols = outs[0].shape
        for g in range(group_count):
            rounded = total[:, column : column + cols].astype(BF16)
            column += cols
            for i, out_ref in enumerate(outs):
                out_ref[g] = rounded[i * span_rows : (i + 1) * span_rows]
        floats = rounded.astype(F32)
        squares = jnp.sum(floats * floats, axis=-1, keepdims=True)
        for t in range(squares.shape[0] // HD):
            tile = jnp.broadcast_to(squares[t * HD : (t + 1) * HD], (HD, HD))
            square_ref[n, t : t + 1, :] = tile.T[0:1, :]


def project(normed, weights, layout, indices, groups, begun=None, spans=0):
    _, rows, width = normed.shape
    local = weights[0].shape[-1]
    cols = sum(groups) * local
    anywhere = pl.BlockSpec(memory_space=pl.ANY)
    in_vmem = pl.BlockSpec(memory_space=pltpu.VMEM)
    if spans:
        out_shape = [
            jax.ShapeDtypeStruct((count, rows // spans, local), BF16)
            for count in groups
            for _ in range(spans)
        ]
        out_shape.append(jax.ShapeDtypeStruct((len(groups), rows // HD, HD), F32))
    else:
        out_shape = [jax.ShapeDtypeStruct((rows, cols), F32)]
    result = pl.pallas_call(
        functools.partial(project_kernel, layout, begun is not None, groups, spans),
        in_specs=[pl.BlockSpec(memory_space=pltpu.SMEM)]
        + [anywhere] * (1 + len(weights) + (begun is not None)),
        out_specs=[in_vmem] * len(out_shape),
        out_shape=out_shape,
        scratch_shapes=(
            [pltpu.VMEM((rows, cols), F32), pltpu.SemaphoreType.DMA] if begun is not None else []
        )
        + [
            pltpu.VMEM((rows, len(layout) * width), BF16),
            pltpu.VMEM((len(layout) * width, cols), BF16),
            pltpu.SemaphoreType.DMA((len(layout),)),
            pltpu.SemaphoreType.DMA((len(layout), max(len(block) for block in layout))),
        ],
        compiler_params=params(),
        cost_estimate=cost(
            flops=2 * len(layout) * rows * width * cols,
            bytes_accessed=2 * len(layout) * (rows + cols) * width + 4 * rows * cols,
        ),
        name="project_final" if spans else "project_begin",
    )(indices, normed, *weights, *([begun] if begun is not None else []))
    if not spans:
        return result[0]
    sets = [result[n * spans : (n + 1) * spans] for n in range(len(groups))]
    return (*sets, result[-1])


def attention_kernel(
    total_width, span, places, seen_ref, q_ref, q_gain_ref, k_gain_ref, k0, k1, k2, v0, v1, v2, *refs
):
    *square_refs, out_ref = refs
    rows, cols = q_ref.shape
    tiles = rows // HD
    factors = []
    for array, first in places:
        pieces = []
        for t in range(tiles):
            row = sum(ref[array, first + t : first + t + 1, :] for ref in square_refs)
            pieces.append(jnp.broadcast_to(row, (HD, HD)).T[:, 0:1])
        squares = jnp.concatenate(pieces, axis=0)
        factors.append(lax.rsqrt(squares / total_width + 1e-06))
    hide = [jnp.where(seen_ref[span, w] == 1, 0.0, 1e30).astype(F32) for w in range(2)] + [0.0]
    to_exponent = HD ** (-0.5) * math.log2(math.e)

    def with_gain(ref, head, factor, gain_ref):
        values = ref[:, head].astype(F32) * factor * gain_ref[:, head]
        return values.astype(BF16)

    def scores_of(head):
        query = with_gain(q_ref, head, factors[0], q_gain_ref)
        return [
            lax.dot_general(
                query,
                with_gain(key, head, factors[1 + w], k_gain_ref),
                (((1,), (1,)), ((), ())),
                preferred_element_type=F32,
            )
            for w, key in enumerate((k0, k1, k2))
        ]

    heads = [slice(h * HD, (h + 1) * HD) for h in range(cols // HD)]
    scores = scores_of(heads[0])
    for h, head in enumerate(heads):
        following = scores_of(heads[h + 1]) if h + 1 < len(heads) else None
        tops = [jnp.max(s, axis=-1, keepdims=True) for s in scores]
        top = functools.reduce(jnp.maximum, (m - x for m, x in zip(tops, hide)))
        expos = [
            jnp.exp2(s * to_exponent - (top * to_exponent + x)) for s, x in zip(scores, hide)
        ]
        inverse = 1.0 / jnp.sum(expos[0] + expos[1] + expos[2], axis=-1, keepdims=True)
        total = None
        for expo, value in zip(expos, (v0, v1, v2)):
            probs = (expo * inverse).astype(BF16)
            term = jnp.dot(probs, value[:, head], preferred_element_type=F32)
            total = term if total is None else total + term
        out_ref[:, head] = total.astype(BF16)
        scores = following


def attend(span, seen, query, squares, gains, prior, own, total_width):
    spans = len(own)
    _, rows, cols = query.shape
    heads = cols // HD
    tiles = rows // HD
    window = [(spans + span - 2 + w) for w in range(3)]
    window = [(0 if position >= spans else 2, position % spans) for position in window]
    places = [(1, span * tiles)] + [(array, index * tiles) for array, index in window]
    arrays = [(own if array == 0 else prior)[index] for array, index in window]

    def part(which):
        return pl.BlockSpec((None, rows, cols), lambda i: (which, 0, 0))

    gain_spec = pl.BlockSpec((1, cols), lambda i: (0, 0))
    return pl.pallas_call(
        functools.partial(attention_kernel, total_width, span, places),
        grid=(1,),
        in_specs=[pl.BlockSpec(memory_space=pltpu.SMEM), part(0), gain_spec, gain_spec]
        + [part(1)] * 3
        + [part(0)] * 3
        + [pl.BlockSpec(memory_space=pltpu.VMEM)] * len(squares),
        out_specs=pl.BlockSpec((rows, cols), lambda i: (0, 0)),
        out_shape=jax.ShapeDtypeStruct((rows, cols), BF16),
        compiler_params=params(),
        cost_estimate=cost(
            flops=12 * rows * rows * cols,
            bytes_accessed=16 * rows * cols,
            transcendentals=3 * rows * rows * heads,
        ),
        name="attend",
    )(seen, query, *gains, *arrays, *arrays, *squares)


def along_line(value, axis):
    count = lax.axis_size(axis)

    def move(moved, by, least):
        pairs = [(i, i + by) for i in range(count) if 0 <= i + by < count]
        if least:
            pairs = [(i, j) for i, j in pairs if 0 <= i - by < count]
        return lax.ppermute(moved, axis, pairs)

    below = {1: move(value, 1, 0)}
    above = {1: move(value, -1, 0)}
    for k in range(3, count):
        pairs = [(i, i + s * k) for i in range(count) for s in (1, -1) if 0 <= i + s * k < count]
        if 2 * k >= count and count < 2 * k + 1 and len({j for _, j in pairs}) == len(pairs):
            below[k] = above[k] = lax.ppermute(value, axis, pairs)
        else:
            below[k] = move(value, k, 0)
            above[k] = move(value, -k, 0)
    if count > 2:
        below[2] = move(below[1], 1, 1)
        above[2] = move(above[1], -1, 1)
    return [value] + [below[k] for k in range(1, count)] + [above[k] for k in range(1, count)]


def late_slots(groups):
    return sorted({2, groups - 2}) if groups > 2 else []


class Fetch:
    def __init__(self, place_ref, span, line, weight_ref, scratch):
        self.attended, self.weights, self.sems = scratch[:3]
        self.groups = (len(line) + 1) // 2
        self.mine, self.span, self.place_ref = place_ref[0], span, place_ref
        self.line, self.weight_ref, self.columns_scratch = line, weight_ref, scratch[3:]

    def slot(self, i, source):
        return pltpu.make_async_copy(source, self.attended.at[i], self.sems.at[0, i])

    def start_attended(self, slots):
        below, above = self.line[1 : self.groups], self.line[self.groups :]
        for i, k in enumerate(slots):
            if k == 0:
                self.slot(i, self.line[0]).start()
                continue

            @pl.when(self.mine >= k)
            def _():
                self.slot(i, below[k - 1]).start()

            @pl.when(self.mine < k)
            def _():
                self.slot(i, above[self.groups - k - 1]).start()

    def start_weights(self, slots, stacks=()):
        for i, k in enumerate(slots):
            group = lax.rem(self.mine + self.groups - k, self.groups)
            if not stacks:
                pltpu.make_async_copy(
                    self.weight_ref.at[group], self.weights.at[i], self.sems.at[1, i]
                ).start()
                continue
            count, _, sharers, part, cols = stacks[0].shape
            first = self.place_ref.shape[0] - count * len(stacks)
            for n in range(count * len(stacks)):
                row = pl.multiple_of(self.place_ref[first + n] * part, part)
                for o in range(sharers):
                    pltpu.make_async_copy(
                        stacks[n // count].at[n % count, group, o],
                        self.weights.at[i, pl.ds(row, part), pl.ds(o * cols, cols)],
                        self.sems.at[1, i],
                    ).start()

    def wait_weight(self, i):
        pltpu.make_async_copy(self.weights.at[i], self.weights.at[i], self.sems.at[1, i]).wait()

    def columns(self, latents_ref, control_ref, mod_ref):
        latents, control, mods = self.columns_scratch
        width = latents.shape[1]
        columns = pl.ds(pl.multiple_of(self.mine * width, HD), width)
        rows = pl.ds(pl.multiple_of(self.place_ref[1 + self.span] // 8 * 8, 8), 8)
        sources = (
            latents_ref.at[self.span, :, columns],
            control_ref.at[self.span, :, columns],
            mod_ref.at[2, rows, columns],
        )
        return [
            pltpu.make_async_copy(source, target, self.sems.at[2, i])
            for i, (source, target) in enumerate(zip(sources, (latents, control, mods)))
        ]

    def branch(self, slots, new_weights, total=None):
        for i, k in enumerate(slots):
            self.slot(i, self.line[0]).wait()

            @pl.when(new_weights)
            def _():
                self.wait_weight(i)

            part = jnp.dot(self.attended[i], self.weights[i], preferred_element_type=F32)
            part = part.astype(BF16).astype(F32)
            total = part if total is None else total + part
        return total

    def updated(self, branch, columns):
        latents, control, mods = self.columns_scratch
        for copy in columns:
            copy.wait()
        hidden = latents[...].astype(F32) + control[...].astype(F32)
        return hidden + mods[pl.ds(lax.rem(self.place_ref[1 + self.span], 8), 1), :] * branch


def start_all(copies):
    for copy in copies:
        copy.start()


def last_kernel(span, count, place_ref, latents_ref, control_ref, mod_ref, *refs):
    line, out_ref, scratch = refs[count:-7], refs[-7], refs[-6:]
    fetch = Fetch(place_ref, span, line, refs[0], scratch)
    slots = range(fetch.groups)
    columns = fetch.columns(latents_ref, control_ref, mod_ref)
    fetch.start_attended(slots)
    fetch.start_weights(slots, refs[:count] if count > 1 else ())
    start_all(columns)
    out_ref[...] = fetch.updated(fetch.branch(slots, True), columns).astype(BF16)


def begin_kernel(slots, place_ref, weight_ref, *refs):
    line, out_ref, scratch = refs[:-4], refs[-4], refs[-3:]
    span = pl.program_id(0)
    rows = out_ref.shape[1]
    mine = [ref.at[pl.ds(pl.multiple_of(span * rows, rows), rows)] for ref in line]
    fetch = Fetch(place_ref, span, mine, weight_ref, scratch)
    fetch.start_attended(slots)

    @pl.when(span == 0)
    def _():
        fetch.start_weights(slots)

    out_ref[0] = fetch.branch(slots, span == 0)


def rest_kernel(
    slots, place_ref, arrived_ref, begun_ref, weight_ref, latents_ref, control_ref, mod_ref, *refs
):
    line, out_ref, scratch = refs[:-7], refs[-7], refs[-6:]
    step = pl.program_id(0)
    rows = out_ref.shape[1]

    def of_span(span):
        mine = [ref.at[pl.ds(pl.multiple_of(span * rows, rows), rows)] for ref in line]
        fetch = Fetch(place_ref, span, mine, weight_ref, scratch)
        return fetch, fetch.columns(latents_ref, control_ref, mod_ref)

    @pl.when(step == 0)
    def _():
        fetch, columns = of_span(0)
        fetch.start_attended(slots)
        fetch.start_weights(slots)
        start_all(columns)
        out_ref[0] = arrived_ref[...].astype(F32)

    @pl.when(step > 0)
    def _():
        fetch, columns = of_span(step - 1)

        @pl.when(step > 1)
        def _():
            fetch.start_attended(slots)
            start_all(columns)

        branch = fetch.branch(slots, step == 1, begun_ref[0])
        out_ref[0] = fetch.updated(branch, columns)


def update_scratch(slots, rows, cols, width, columns=True):
    scratch = [
        pltpu.VMEM((len(slots), rows, cols), BF16),
        pltpu.VMEM((len(slots), cols, width), BF16),
        pltpu.SemaphoreType.DMA((3, max(len(slots), 3))),
    ]
    if columns:
        scratch.append(pltpu.VMEM((rows, width), BF16))
        scratch.append(pltpu.VMEM((rows, width), BF16))
        scratch.append(pltpu.VMEM((8, width), F32))
    return scratch


def update_cost(slots, rows, cols, width):
    return cost(
        flops=2 * slots * rows * cols * width,
        bytes_accessed=2 * slots * cols * (rows + width) + 8 * rows * width,
    )


def update_last(place, line, weights, latents, control, modulation, width):
    rows, cols = line[0].shape
    groups = (len(line) + 1) // 2
    span = latents.shape[0] - 1
    anywhere = pl.BlockSpec(memory_space=pl.ANY)
    return pl.pallas_call(
        functools.partial(last_kernel, span, len(weights)),
        in_specs=[pl.BlockSpec(memory_space=pltpu.SMEM)]
        + [anywhere] * (3 + len(weights) + len(line)),
        out_specs=pl.BlockSpec(memory_space=pltpu.VMEM),
        scratch_shapes=update_scratch(range(groups), rows, cols, width),
        out_shape=jax.ShapeDtypeStruct((rows, width), BF16),
        compiler_params=params(),
        cost_estimate=update_cost(groups, rows, cols, width),
        name="update_last",
    )(place, latents, control, modulation, *weights, *line)


def update_begin(place, line, weights, spans, rows, slots):
    cols = line[0].shape[1]
    width = weights.shape[2]
    anywhere = pl.BlockSpec(memory_space=pl.ANY)
    return pl.pallas_call(
        functools.partial(begin_kernel, slots),
        grid=(spans - 1,),
        in_specs=[pl.BlockSpec(memory_space=pltpu.SMEM)] + [anywhere] * (1 + len(line)),
        out_specs=pl.BlockSpec((1, rows, width), lambda i: (i, 0, 0)),
        scratch_shapes=update_scratch(slots, rows, cols, width, columns=False),
        out_shape=jax.ShapeDtypeStruct((spans - 1, rows, width), F32),
        compiler_params=params(),
        cost_estimate=update_cost(len(slots) * (spans - 1), rows, cols, width),
        name="update_begin",
    )(place, weights, *line)


def update_rest(place, arrived, line, weights, latents, control, modulation):
    cols = line[0].shape[1]
    spans, rows, _ = latents.shape
    groups, _, width = weights.shape
    late = late_slots(groups) or [groups - 1]
    early = [k for k in range(groups) if k not in late]
    ready = list(line)
    for k in late:
        ready[k] = ready[groups - 1 + k] = line[0]
    begun = update_begin(place, ready, weights, spans, rows, early)
    anywhere = pl.BlockSpec(memory_space=pl.ANY)
    return pl.pallas_call(
        functools.partial(rest_kernel, late),
        grid=(spans,),
        in_specs=[
            pl.BlockSpec(memory_space=pltpu.SMEM),
            pl.BlockSpec((rows, width), lambda i: (0, 0)),
            pl.BlockSpec((1, rows, width), lambda i: (jnp.maximum(i - 1, 0), 0, 0)),
        ]
        + [anywhere] * (4 + len(line)),
        out_specs=pl.BlockSpec((1, rows, width), lambda i: (i, 0, 0)),
        scratch_shapes=update_scratch(late, rows, cols, width),
        out_shape=jax.ShapeDtypeStruct((spans, rows, width), F32),
        compiler_params=params(),
        cost_estimate=update_cost(len(late) * (spans - 1), rows, cols, width),
        name="update_rest",
    )(place, arrived, begun, weights, latents, control, modulation, *line)


def out_shares(w_out):
    owners = lax.axis_size("queue")
    rows, cols = w_out.shape
    return lax.all_to_all(w_out.reshape(owners, rows // owners, cols), "queue", 0, 0, tiled=True)


def out_blocks(shares):
    groups = lax.axis_size("head")
    owners, part, cols = shares.shape
    blocks = lax.all_to_all(shares, "head", 0, 0, tiled=True)
    return blocks.reshape(groups, owners // groups, part, cols)


def assemble_kernel(index_ref, *refs):
    *stacks, out_ref, sems = refs
    count, groups, sharers, part, cols = stacks[0].shape
    copies = []
    for i, stack in enumerate(stacks):
        for b in range(count):
            start = pl.multiple_of(index_ref[i * count + b] * part, part)
            for g in range(groups):
                for o in range(sharers):
                    copy = pltpu.make_async_copy(
                        stack.at[b, g, o],
                        out_ref.at[g, pl.ds(start, part), pl.ds(o * cols, cols)],
                        sems.at[i * count + b, g, o],
                    )
                    copy.start()
                    copies.append(copy)
    for copy in copies:
        copy.wait()


def assemble(stacks, indices):
    count, groups, sharers, part, cols = stacks[0].shape
    blocks = count * len(stacks)
    return pl.pallas_call(
        assemble_kernel,
        in_specs=[pl.BlockSpec(memory_space=pltpu.SMEM)]
        + [pl.BlockSpec(memory_space=pl.ANY)] * len(stacks),
        out_specs=pl.BlockSpec(memory_space=pltpu.VMEM),
        out_shape=jax.ShapeDtypeStruct((groups, blocks * part, sharers * cols), BF16),
        scratch_shapes=[pltpu.SemaphoreType.DMA((blocks, groups, sharers))],
        compiler_params=params(),
        cost_estimate=cost(flops=0, bytes_accessed=4 * stacks[0].size * len(stacks)),
        name="assemble",
    )(jnp.stack(indices), *stacks)


def assemble_in_order(gathered):
    owners, groups, sharers, part, cols = gathered.shape
    shape = (groups, owners * part, sharers * cols)
    return gathered.transpose(1, 0, 3, 2, 4).reshape(shape)


def shards(
    latents,
    control,
    levels,
    window_mask,
    modulation,
    w_query,
    w_key,
    w_value,
    w_out,
    q_gain,
    k_gain,
):
    spans, row_count, _ = latents.shape
    local_cols = w_query.shape[1]
    owners = lax.axis_size("queue")
    total_width = local_cols * lax.axis_size("head")
    owner_index = lax.axis_index("queue")
    head_index = lax.axis_index("head")
    mine = owner_index.astype(jnp.int32)
    block_indices = [mine ^ m ^ c for c in range(2) for m in (0, 2, 4, 6)]
    place = jnp.concatenate(
        [head_index.astype(jnp.int32).reshape(1), levels, jnp.stack(block_indices)]
    )
    modulation = modulation.transpose(1, 0, 2)
    gain_rows = [gain.reshape(1, -1) for gain in (q_gain, k_gain)]
    cube = is_cube(w_query.shape[0], local_cols) and w_out.shape[0] // owners % 16 == 0
    span_ids = owner_index * spans + jnp.arange(spans, dtype=jnp.int32)
    seen = (
        (window_mask == 1) & (span_ids[:, None] >= jnp.array([2, 1], jnp.int32)[None, :])
    ).astype(jnp.int32)

    if cube:
        mine = owner_index.astype(jnp.int32)
        high = w_query.shape[0]

        def indices(masks):
            return jnp.stack([mine ^ m for m in masks])

        halves_of = halves(w_query)
        sides = (jnp.concatenate([w_value, halves_of[0]]), jnp.concatenate([halves_of[1], w_key]))
        firsts = [{m: exchange(side, m) for m in (2, 4)} for side in sides]
        early, late = [0, 1, 2, 4, 3, 5], [6, 7]
        early_indices, late_indices = indices(early), indices(late)
        small = (seen, place, early_indices, late_indices, *gain_rows)
        normed = modulated_norm(after(latents, *small), control, levels, modulation, owners)
        firsts[0][4], firsts[1][2] = after(firsts[0][4], normed), after(firsts[1][2], normed)
        for side, first in zip(sides, firsts):
            first.update({0: side, 1: exchange(after(side, normed), 1)})
        share = out_shares(after(w_out, normed, firsts[0][4], firsts[1][2]))
        across = [
            exchange(after(firsts[0][4], normed, share), 2),
            exchange(after(firsts[1][2], normed, share), 4),
        ]
        firsts[0][2] = after(firsts[0][2], normed, share)
        firsts[1][4] = after(firsts[1][4], normed, share)
        firsts = [second_step(first) for first in firsts]
        columns = {"value": 0, "key": local_cols, "query": 2 * local_cols}
        half = high // 2

        def layout_of(count):
            return tuple(
                (
                    (2 * b, 0, high, 0, columns["value"]),
                    (2 * b, high, half, 0, columns["query"]),
                    (2 * b + 1, 0, half, half, columns["query"]),
                    (2 * b + 1, half, high, 0, columns["key"]),
                )
                for b in range(count)
            )

        parts = [first[m] for m in early for first in firsts]
        begun = project(normed, parts, layout_of(len(early)), early_indices, (3,))
        across = [after(part, begun) for part in across]
        parts = across + [exchange(part, 1) for part in across]
        own, query, squares = project(
            normed,
            parts,
            layout_of(len(late)),
            late_indices,
            (2, 1),
            begun=begun,
            spans=spans,
        )
    else:
        normed = modulated_norm(latents, control, levels, modulation, 1)
        weights = [
            lax.all_gather(w, "queue", axis=0, tiled=True) for w in (w_value, w_key, w_query)
        ]
        model = weights[0].shape[0]
        layout = (tuple((w, 0, model, 0, w * local_cols) for w in range(3)),)
        zero = jnp.zeros((1,), jnp.int32)
        own, query, squares = project(normed, weights, layout, zero, (2, 1), spans=spans)
        share = out_shares(w_out)

    prior = [from_behind(span, "queue", 1) for span in reversed(own)][::-1]
    prior_squares = from_behind(squares, "queue", 1)
    share = out_blocks(after(share, prior_squares)) if cube else out_blocks(share)
    squares = sum_terms(jnp.concatenate([squares, prior_squares]), "head")

    def attended_of(span, ready):
        return attend(span, seen, ready, squares, gain_rows, prior, own, total_width)

    groups = lax.axis_size("head")
    attended_last = attended_of(spans - 1, query[-1])
    last = along_line(attended_last, "head")
    sent = [last[1], last[groups]]
    begin_rest = [attended_last, *sent]
    if cube:
        share = after(share, *squares)
        first = {m: exchange(share, m) for m in (2, 4)}
    rest = [attended_of(span, after(query[span], *begin_rest)) for span in range(spans - 1)]
    rest = rest[0] if len(rest) == 1 else jnp.concatenate(rest, axis=0)
    line = along_line(rest, "head")
    if cube:
        first = {m: after(block, rest, *prior) for m, block in first.items()}
        half = share.shape[0] // 2
        across = [exchange(first[4][:half], 2), exchange(first[2][half:], 4)]
        across = jnp.concatenate([after(part, *last[1:]) for part in across])
        mine_blocks = jnp.stack([share, first[2], first[4], across])
        swapped = exchange(mine_blocks, 1)
        parts = [mine_blocks, swapped]
    else:
        weights = assemble_in_order(lax.all_gather(share, "queue", axis=0))
        parts = [weights]
    rest = line
    width = latents.shape[2] // groups
    updated_last = update_last(place, last, parts, latents, control, modulation, width)
    if cube:
        swapped = after(swapped, updated_last, rest[1], rest[groups])
        weights = assemble([mine_blocks, swapped], block_indices)
    arrived = shifted(updated_last, "queue", 1)
    return update_rest(place, arrived, rest, weights, latents, control, modulation)


def solution(mesh):
    placed = (
        P("queue", None, None),
        P("queue", None, None),
        P("queue"),
        P("queue", None),
        P(),
        P("queue", "head"),
        P("queue", "head"),
        P("queue", "head"),
        P("head", "queue"),
        P("head"),
        P("head"),
    )
    return jax.shard_map(
        shards, mesh=mesh, in_specs=placed, out_specs=P("queue", None, "head"), check_vma=False
    )
```

```python
import functools
import math

import jax
import jax.numpy as jnp
from jax import lax
from jax.experimental import pallas as pl
from jax.experimental.pallas import tpu as pltpu
from jax.sharding import PartitionSpec as P

HD = 128
F32 = jnp.float32
BF16 = jnp.bfloat16
VMEM_BYTES = 60 * 1024 * 1024
WEIGHT = 16


def params():
    return pltpu.CompilerParams(vmem_limit_bytes=VMEM_BYTES)


def cost(flops, bytes_accessed, transcendentals=0):
    return pl.CostEstimate(
        flops=flops // WEIGHT,
        bytes_accessed=bytes_accessed // WEIGHT,
        transcendentals=transcendentals // WEIGHT,
    )


def from_behind(value, axis, by):
    peers = lax.axis_size(axis)
    pairs = [(i, i + by) for i in range(peers) if 0 <= i + by < peers]
    return lax.ppermute(value, axis, pairs)


def shifted(value, axis, steps):
    count = lax.axis_size(axis)
    pairs = [(source, (source + steps) % count) for source in range(count)]
    return lax.ppermute(value, axis, pairs)


def after(value, *others):
    return lax.optimization_barrier((value, *others))[0]


def sum_terms(value, axis):
    count = lax.axis_size(axis)
    if count & (count - 1):
        return [value] + [shifted(value, axis, steps) for steps in range(1, count)]
    terms, bit = [value], 1
    while bit < count:
        total = functools.reduce(jnp.add, terms)
        terms = [total, lax.ppermute(total, axis, [(i, i ^ bit) for i in range(count)])]
        bit *= 2
    return terms


def is_cube(row_count, col_count):
    return lax.axis_size("queue") == 2**3 and row_count % 32 == 0 and col_count % HD == 0


def exchange(value, bit):
    peers = lax.axis_size("queue")
    return lax.ppermute(value, "queue", [(i, i ^ bit) for i in range(peers)])


def first_step(block):
    return {0: block, 1: exchange(block, 1), 2: exchange(block, 2), 4: exchange(block, 4)}


def second_step(first):
    return {**first, 3: exchange(first[2], 1), 5: exchange(first[4], 1)}


def halves(block):
    half = block.shape[0] // 2
    return block[:half], block[half:]


def norm_kernel(levels_ref, latents_ref, control_ref, mod_ref, out_ref):
    blocks, _, width = out_ref.shape
    hidden = latents_ref[0].astype(F32) + control_ref[0].astype(F32)
    center = hidden - jnp.mean(hidden, axis=-1, keepdims=True)
    variance = jnp.mean(center * center, axis=-1, keepdims=True)
    normed = center * lax.rsqrt(variance + 1e-06)
    row = lax.rem(levels_ref[pl.program_id(0)], 8)
    normed = normed * (1.0 + mod_ref[1, pl.ds(row, 1), :]) + mod_ref[0, pl.ds(row, 1), :]
    normed = normed.astype(BF16)
    for j in range(blocks):
        out_ref[j] = normed[:, j * width : (j + 1) * width]


def modulated_norm(latents, control, levels, modulation, blocks):
    spans, rows, model = latents.shape
    tile = 128 if rows % 128 == 0 else rows
    tiles = rows // tile
    width = model // blocks
    return pl.pallas_call(
        norm_kernel,
        grid_spec=pltpu.PrefetchScalarGridSpec(
            num_scalar_prefetch=1,
            grid=(spans, tiles),
            in_specs=[
                pl.BlockSpec((1, tile, model), lambda s, t, lev: (s, t, 0)),
                pl.BlockSpec((1, tile, model), lambda s, t, lev: (s, t, 0)),
                pl.BlockSpec((2, 8, model), lambda s, t, lev: (0, lev[s] // 8, 0)),
            ],
            out_specs=pl.BlockSpec((blocks, tile, width), lambda s, t, lev: (0, s * tiles + t, 0)),
        ),
        out_shape=jax.ShapeDtypeStruct((blocks, spans * rows, width), BF16),
        compiler_params=params(),
        cost_estimate=cost(
            flops=10 * latents.size, bytes_accessed=6 * latents.size, transcendentals=0
        ),
        name="modulated_norm",
    )(levels, latents, control, modulation)


def project_kernel(layout, begun, groups, spans, *refs):
    refs = list(refs)
    index_ref = refs.pop(0)
    normed_ref = refs.pop(0)
    count = 1 + max(piece[0] for block in layout for piece in block)
    weight_refs = [refs.pop(0) for _ in range(count)]
    begun_ref = refs.pop(0) if begun else None
    *out_refs, rows_buf, weight_buf, row_sems, weight_sems = refs
    if begun:
        *out_refs, begun_buf, begun_sem = out_refs
    width = normed_ref.shape[2]

    def copies_of(b):
        copies = [
            pltpu.make_async_copy(
                normed_ref.at[index_ref[b]],
                rows_buf.at[:, pl.ds(b * width, width)],
                row_sems.at[b],
            )
        ]
        for p, (operand, first, high, row, col) in enumerate(layout[b]):
            source = weight_refs[operand]
            target = weight_buf.at[pl.ds(b * width + row, high), pl.ds(col, source.shape[1])]
            copies.append(
                pltpu.make_async_copy(source.at[pl.ds(first, high)], target, weight_sems.at[b, p])
            )
        return copies

    pairs = [range(b, min(b + 2, len(layout))) for b in range(0, len(layout), 2)]
    copies = [sum((copies_of(b) for b in pair), []) for pair in pairs]
    for ahead in copies[:2]:
        for copy in ahead:
            copy.start()
    if begun:
        fetch_begun = pltpu.make_async_copy(begun_ref, begun_buf, begun_sem)
        fetch_begun.start()
    total = None
    for i, pair in enumerate(pairs):
        for copy in copies[i]:
            copy.wait()
        if i + 2 < len(pairs):
            for copy in copies[i + 2]:
                copy.start()
        span = slice(pair[0] * width, (pair[-1] + 1) * width)
        term = jnp.dot(rows_buf[:, span], weight_buf[span], preferred_element_type=F32)
        total = term if total is None else total + term
    if begun:
        fetch_begun.wait()
        total = total + begun_buf[...]
    if not spans:
        out_refs[0][...] = total
        return
    *out_refs, square_ref = out_refs
    column = 0
    for n, group_count in enumerate(groups):
        out_ref = out_refs[n]
        _, _, span_rows, cols = out_ref.shape
        for g in range(group_count):
            rounded = total[:, column : column + cols].astype(BF16)
            column += cols
            for i in range(spans):
                out_ref[i, g] = rounded[i * span_rows : (i + 1) * span_rows]
        floats = rounded.astype(F32)
        squares = jnp.sum(floats * floats, axis=-1, keepdims=True)
        for t in range(squares.shape[0] // HD):
            tile = jnp.broadcast_to(squares[t * HD : (t + 1) * HD], (HD, HD))
            square_ref[n, t : t + 1, :] = tile.T[0:1, :]


def project(normed, weights, layout, indices, groups, begun=None, spans=0):
    _, rows, width = normed.shape
    local = weights[0].shape[-1]
    cols = sum(groups) * local
    anywhere = pl.BlockSpec(memory_space=pl.ANY)
    in_vmem = pl.BlockSpec(memory_space=pltpu.VMEM)
    if spans:
        out_shape = [
            jax.ShapeDtypeStruct((spans, count, rows // spans, local), BF16) for count in groups
        ]
        out_shape.append(jax.ShapeDtypeStruct((len(groups), rows // HD, HD), F32))
    else:
        out_shape = [jax.ShapeDtypeStruct((rows, cols), F32)]
    result = pl.pallas_call(
        functools.partial(project_kernel, layout, begun is not None, groups, spans),
        in_specs=[pl.BlockSpec(memory_space=pltpu.SMEM)]
        + [anywhere] * (1 + len(weights) + (begun is not None)),
        out_specs=[in_vmem] * len(out_shape),
        out_shape=out_shape,
        scratch_shapes=(
            [pltpu.VMEM((rows, cols), F32), pltpu.SemaphoreType.DMA] if begun is not None else []
        )
        + [
            pltpu.VMEM((rows, len(layout) * width), BF16),
            pltpu.VMEM((len(layout) * width, cols), BF16),
            pltpu.SemaphoreType.DMA((len(layout),)),
            pltpu.SemaphoreType.DMA((len(layout), max(len(block) for block in layout))),
        ],
        compiler_params=params(),
        cost_estimate=cost(
            flops=2 * len(layout) * rows * width * cols,
            bytes_accessed=2 * len(layout) * (rows + cols) * width + 4 * rows * cols,
        ),
        name="project_final" if spans else "project_begin",
    )(indices, normed, *weights, *([begun] if begun is not None else []))
    return result if spans else result[0]


def attention_kernel(
    total_width, span, places, seen_ref, q_ref, q_gain_ref, k_gain_ref, k0, k1, k2, v0, v1, v2, *refs
):
    *square_refs, out_ref = refs
    rows, cols = q_ref.shape
    tiles = rows // HD
    factors = []
    for array, first in places:
        pieces = []
        for t in range(tiles):
            row = sum(ref[array, first + t : first + t + 1, :] for ref in square_refs)
            pieces.append(jnp.broadcast_to(row, (HD, HD)).T[:, 0:1])
        squares = jnp.concatenate(pieces, axis=0)
        factors.append(lax.rsqrt(squares / total_width + 1e-06))
    hide = [jnp.where(seen_ref[span, w] == 1, 0.0, 1e30).astype(F32) for w in range(2)] + [0.0]
    to_exponent = HD ** (-0.5) * math.log2(math.e)

    def with_gain(ref, head, factor, gain_ref):
        values = ref[:, head].astype(F32) * factor * gain_ref[:, head]
        return values.astype(BF16)

    def scores_of(head):
        query = with_gain(q_ref, head, factors[0], q_gain_ref)
        return [
            lax.dot_general(
                query,
                with_gain(key, head, factors[1 + w], k_gain_ref),
                (((1,), (1,)), ((), ())),
                preferred_element_type=F32,
            )
            for w, key in enumerate((k0, k1, k2))
        ]

    heads = [slice(h * HD, (h + 1) * HD) for h in range(cols // HD)]
    scores = scores_of(heads[0])
    for h, head in enumerate(heads):
        following = scores_of(heads[h + 1]) if h + 1 < len(heads) else None
        tops = [jnp.max(s, axis=-1, keepdims=True) for s in scores]
        top = functools.reduce(jnp.maximum, (m - x for m, x in zip(tops, hide)))
        expos = [
            jnp.exp2(s * to_exponent - (top * to_exponent + x)) for s, x in zip(scores, hide)
        ]
        inverse = 1.0 / jnp.sum(expos[0] + expos[1] + expos[2], axis=-1, keepdims=True)
        total = None
        for expo, value in zip(expos, (v0, v1, v2)):
            probs = (expo * inverse).astype(BF16)
            term = jnp.dot(probs, value[:, head], preferred_element_type=F32)
            total = term if total is None else total + term
        out_ref[:, head] = total.astype(BF16)
        scores = following


def attend(span, seen, query, squares, gains, prior, own, total_width):
    spans, _, rows, cols = query.shape
    heads = cols // HD
    tiles = rows // HD
    window = [(spans + span - 2 + w) for w in range(3)]
    window = [(0 if position >= spans else 2, position % spans) for position in window]
    places = [(1, span * tiles)] + [(array, index * tiles) for array, index in window]
    arrays = [own if array == 0 else prior for array, _ in window]

    def part(which, index):
        return pl.BlockSpec((None, None, rows, cols), lambda i: (index, which, 0, 0))

    gain_spec = pl.BlockSpec((1, cols), lambda i: (0, 0))
    return pl.pallas_call(
        functools.partial(attention_kernel, total_width, span, places),
        grid=(1,),
        in_specs=[pl.BlockSpec(memory_space=pltpu.SMEM), part(0, span), gain_spec, gain_spec]
        + [part(1, index) for _, index in window]
        + [part(0, index) for _, index in window]
        + [pl.BlockSpec(memory_space=pltpu.VMEM)] * len(squares),
        out_specs=pl.BlockSpec((rows, cols), lambda i: (0, 0)),
        out_shape=jax.ShapeDtypeStruct((rows, cols), BF16),
        compiler_params=params(),
        cost_estimate=cost(
            flops=12 * rows * rows * cols,
            bytes_accessed=16 * rows * cols,
            transcendentals=3 * rows * rows * heads,
        ),
        name="attend",
    )(seen, query, *gains, *arrays, *arrays, *squares)


def along_line(value, axis):
    count = lax.axis_size(axis)

    def move(moved, by, least):
        pairs = [(i, i + by) for i in range(count) if 0 <= i + by < count]
        if least:
            pairs = [(i, j) for i, j in pairs if 0 <= i - by < count]
        return lax.ppermute(moved, axis, pairs)

    below = {1: move(value, 1, 0)}
    above = {1: move(value, -1, 0)}
    for k in range(3, count):
        pairs = [(i, i + s * k) for i in range(count) for s in (1, -1) if 0 <= i + s * k < count]
        if 2 * k >= count and count < 2 * k + 1 and len({j for _, j in pairs}) == len(pairs):
            below[k] = above[k] = lax.ppermute(value, axis, pairs)
        else:
            below[k] = move(value, k, 0)
            above[k] = move(value, -k, 0)
    if count > 2:
        below[2] = move(below[1], 1, 1)
        above[2] = move(above[1], -1, 1)
    return [value] + [below[k] for k in range(1, count)] + [above[k] for k in range(1, count)]


def late_slots(groups):
    return sorted({2, groups - 2}) if groups > 2 else []


class Fetch:
    def __init__(self, place_ref, span, line, weight_ref, scratch):
        self.attended, self.weights, self.sems = scratch[:3]
        self.groups = (len(line) + 1) // 2
        self.mine, self.span, self.place_ref = place_ref[0], span, place_ref
        self.line, self.weight_ref, self.columns_scratch = line, weight_ref, scratch[3:]

    def slot(self, i, source):
        return pltpu.make_async_copy(source, self.attended.at[i], self.sems.at[0, i])

    def start_attended(self, slots):
        below, above = self.line[1 : self.groups], self.line[self.groups :]
        for i, k in enumerate(slots):
            if k == 0:
                self.slot(i, self.line[0]).start()
                continue

            @pl.when(self.mine >= k)
            def _():
                self.slot(i, below[k - 1]).start()

            @pl.when(self.mine < k)
            def _():
                self.slot(i, above[self.groups - k - 1]).start()

    def start_weights(self, slots, stacks=()):
        for i, k in enumerate(slots):
            group = lax.rem(self.mine + self.groups - k, self.groups)
            if not stacks:
                pltpu.make_async_copy(
                    self.weight_ref.at[group], self.weights.at[i], self.sems.at[1, i]
                ).start()
                continue
            count, _, sharers, part, cols = stacks[0].shape
            first = self.place_ref.shape[0] - count * len(stacks)
            for n in range(count * len(stacks)):
                row = pl.multiple_of(self.place_ref[first + n] * part, part)
                for o in range(sharers):
                    pltpu.make_async_copy(
                        stacks[n // count].at[n % count, group, o],
                        self.weights.at[i, pl.ds(row, part), pl.ds(o * cols, cols)],
                        self.sems.at[1, i],
                    ).start()

    def wait_weight(self, i):
        pltpu.make_async_copy(self.weights.at[i], self.weights.at[i], self.sems.at[1, i]).wait()

    def columns(self, latents_ref, control_ref, mod_ref):
        latents, control, mods = self.columns_scratch
        width = latents.shape[1]
        columns = pl.ds(pl.multiple_of(self.mine * width, HD), width)
        rows = pl.ds(pl.multiple_of(self.place_ref[1 + self.span] // 8 * 8, 8), 8)
        sources = (
            latents_ref.at[self.span, :, columns],
            control_ref.at[self.span, :, columns],
            mod_ref.at[2, rows, columns],
        )
        return [
            pltpu.make_async_copy(source, target, self.sems.at[2, i])
            for i, (source, target) in enumerate(zip(sources, (latents, control, mods)))
        ]

    def branch(self, slots, new_weights, total=None):
        for i, k in enumerate(slots):
            self.slot(i, self.line[0]).wait()

            @pl.when(new_weights)
            def _():
                self.wait_weight(i)

            part = jnp.dot(self.attended[i], self.weights[i], preferred_element_type=F32)
            part = part.astype(BF16).astype(F32)
            total = part if total is None else total + part
        return total

    def updated(self, branch, columns):
        latents, control, mods = self.columns_scratch
        for copy in columns:
            copy.wait()
        hidden = latents[...].astype(F32) + control[...].astype(F32)
        return hidden + mods[pl.ds(lax.rem(self.place_ref[1 + self.span], 8), 1), :] * branch


def start_all(copies):
    for copy in copies:
        copy.start()


def last_kernel(span, count, place_ref, latents_ref, control_ref, mod_ref, *refs):
    line, out_ref, scratch = refs[count:-7], refs[-7], refs[-6:]
    fetch = Fetch(place_ref, span, line, refs[0], scratch)
    slots = range(fetch.groups)
    columns = fetch.columns(latents_ref, control_ref, mod_ref)
    fetch.start_attended(slots)
    fetch.start_weights(slots, refs[:count] if count > 1 else ())
    start_all(columns)
    out_ref[...] = fetch.updated(fetch.branch(slots, True), columns).astype(BF16)


def begin_kernel(slots, place_ref, weight_ref, *refs):
    line, out_ref, scratch = refs[:-4], refs[-4], refs[-3:]
    span = pl.program_id(0)
    rows = out_ref.shape[1]
    mine = [ref.at[pl.ds(pl.multiple_of(span * rows, rows), rows)] for ref in line]
    fetch = Fetch(place_ref, span, mine, weight_ref, scratch)
    fetch.start_attended(slots)

    @pl.when(span == 0)
    def _():
        fetch.start_weights(slots)

    out_ref[0] = fetch.branch(slots, span == 0)


def rest_kernel(
    slots, place_ref, arrived_ref, begun_ref, weight_ref, latents_ref, control_ref, mod_ref, *refs
):
    line, out_ref, scratch = refs[:-7], refs[-7], refs[-6:]
    step = pl.program_id(0)
    rows = out_ref.shape[1]

    def of_span(span):
        mine = [ref.at[pl.ds(pl.multiple_of(span * rows, rows), rows)] for ref in line]
        fetch = Fetch(place_ref, span, mine, weight_ref, scratch)
        return fetch, fetch.columns(latents_ref, control_ref, mod_ref)

    @pl.when(step == 0)
    def _():
        fetch, columns = of_span(0)
        fetch.start_attended(slots)
        fetch.start_weights(slots)
        start_all(columns)
        out_ref[0] = arrived_ref[...].astype(F32)

    @pl.when(step > 0)
    def _():
        fetch, columns = of_span(step - 1)

        @pl.when(step > 1)
        def _():
            fetch.start_attended(slots)
            start_all(columns)

        branch = fetch.branch(slots, step == 1, begun_ref[0])
        out_ref[0] = fetch.updated(branch, columns)


def update_scratch(slots, rows, cols, width, columns=True):
    scratch = [
        pltpu.VMEM((len(slots), rows, cols), BF16),
        pltpu.VMEM((len(slots), cols, width), BF16),
        pltpu.SemaphoreType.DMA((3, max(len(slots), 3))),
    ]
    if columns:
        scratch.append(pltpu.VMEM((rows, width), BF16))
        scratch.append(pltpu.VMEM((rows, width), BF16))
        scratch.append(pltpu.VMEM((8, width), F32))
    return scratch


def update_cost(slots, rows, cols, width):
    return cost(
        flops=2 * slots * rows * cols * width,
        bytes_accessed=2 * slots * cols * (rows + width) + 8 * rows * width,
    )


def update_last(place, line, weights, latents, control, modulation, width):
    rows, cols = line[0].shape
    groups = (len(line) + 1) // 2
    span = latents.shape[0] - 1
    anywhere = pl.BlockSpec(memory_space=pl.ANY)
    return pl.pallas_call(
        functools.partial(last_kernel, span, len(weights)),
        in_specs=[pl.BlockSpec(memory_space=pltpu.SMEM)]
        + [anywhere] * (3 + len(weights) + len(line)),
        out_specs=pl.BlockSpec(memory_space=pltpu.VMEM),
        scratch_shapes=update_scratch(range(groups), rows, cols, width),
        out_shape=jax.ShapeDtypeStruct((rows, width), BF16),
        compiler_params=params(),
        cost_estimate=update_cost(groups, rows, cols, width),
        name="update_last",
    )(place, latents, control, modulation, *weights, *line)


def update_begin(place, line, weights, spans, rows, slots):
    cols = line[0].shape[1]
    width = weights.shape[2]
    anywhere = pl.BlockSpec(memory_space=pl.ANY)
    return pl.pallas_call(
        functools.partial(begin_kernel, slots),
        grid=(spans - 1,),
        in_specs=[pl.BlockSpec(memory_space=pltpu.SMEM)] + [anywhere] * (1 + len(line)),
        out_specs=pl.BlockSpec((1, rows, width), lambda i: (i, 0, 0)),
        scratch_shapes=update_scratch(slots, rows, cols, width, columns=False),
        out_shape=jax.ShapeDtypeStruct((spans - 1, rows, width), F32),
        compiler_params=params(),
        cost_estimate=update_cost(len(slots) * (spans - 1), rows, cols, width),
        name="update_begin",
    )(place, weights, *line)


def update_rest(place, arrived, line, weights, latents, control, modulation):
    cols = line[0].shape[1]
    spans, rows, _ = latents.shape
    groups, _, width = weights.shape
    late = late_slots(groups) or [groups - 1]
    early = [k for k in range(groups) if k not in late]
    ready = list(line)
    for k in late:
        ready[k] = ready[groups - 1 + k] = line[0]
    begun = update_begin(place, ready, weights, spans, rows, early)
    anywhere = pl.BlockSpec(memory_space=pl.ANY)
    return pl.pallas_call(
        functools.partial(rest_kernel, late),
        grid=(spans,),
        in_specs=[
            pl.BlockSpec(memory_space=pltpu.SMEM),
            pl.BlockSpec((rows, width), lambda i: (0, 0)),
            pl.BlockSpec((1, rows, width), lambda i: (jnp.maximum(i - 1, 0), 0, 0)),
        ]
        + [anywhere] * (4 + len(line)),
        out_specs=pl.BlockSpec((1, rows, width), lambda i: (i, 0, 0)),
        scratch_shapes=update_scratch(late, rows, cols, width),
        out_shape=jax.ShapeDtypeStruct((spans, rows, width), F32),
        compiler_params=params(),
        cost_estimate=update_cost(len(late) * (spans - 1), rows, cols, width),
        name="update_rest",
    )(place, arrived, begun, weights, latents, control, modulation, *line)


def out_shares(w_out):
    owners = lax.axis_size("queue")
    rows, cols = w_out.shape
    return lax.all_to_all(w_out.reshape(owners, rows // owners, cols), "queue", 0, 0, tiled=True)


def out_blocks(shares):
    groups = lax.axis_size("head")
    owners, part, cols = shares.shape
    blocks = lax.all_to_all(shares, "head", 0, 0, tiled=True)
    return blocks.reshape(groups, owners // groups, part, cols)


def assemble_kernel(index_ref, *refs):
    *stacks, out_ref, sems = refs
    count, groups, sharers, part, cols = stacks[0].shape
    copies = []
    for i, stack in enumerate(stacks):
        for b in range(count):
            start = pl.multiple_of(index_ref[i * count + b] * part, part)
            for g in range(groups):
                for o in range(sharers):
                    copy = pltpu.make_async_copy(
                        stack.at[b, g, o],
                        out_ref.at[g, pl.ds(start, part), pl.ds(o * cols, cols)],
                        sems.at[i * count + b, g, o],
                    )
                    copy.start()
                    copies.append(copy)
    for copy in copies:
        copy.wait()


def assemble(stacks, indices):
    count, groups, sharers, part, cols = stacks[0].shape
    blocks = count * len(stacks)
    return pl.pallas_call(
        assemble_kernel,
        in_specs=[pl.BlockSpec(memory_space=pltpu.SMEM)]
        + [pl.BlockSpec(memory_space=pl.ANY)] * len(stacks),
        out_specs=pl.BlockSpec(memory_space=pltpu.VMEM),
        out_shape=jax.ShapeDtypeStruct((groups, blocks * part, sharers * cols), BF16),
        scratch_shapes=[pltpu.SemaphoreType.DMA((blocks, groups, sharers))],
        compiler_params=params(),
        cost_estimate=cost(flops=0, bytes_accessed=4 * stacks[0].size * len(stacks)),
        name="assemble",
    )(jnp.stack(indices), *stacks)


def assemble_in_order(gathered):
    owners, groups, sharers, part, cols = gathered.shape
    shape = (groups, owners * part, sharers * cols)
    return gathered.transpose(1, 0, 3, 2, 4).reshape(shape)


def shards(
    latents,
    control,
    levels,
    window_mask,
    modulation,
    w_query,
    w_key,
    w_value,
    w_out,
    q_gain,
    k_gain,
):
    spans, row_count, _ = latents.shape
    local_cols = w_query.shape[1]
    owners = lax.axis_size("queue")
    total_width = local_cols * lax.axis_size("head")
    owner_index = lax.axis_index("queue")
    head_index = lax.axis_index("head")
    mine = owner_index.astype(jnp.int32)
    block_indices = [mine ^ m ^ c for c in range(2) for m in (0, 2, 4, 6)]
    place = jnp.concatenate(
        [head_index.astype(jnp.int32).reshape(1), levels, jnp.stack(block_indices)]
    )
    modulation = modulation.transpose(1, 0, 2)
    gain_rows = [gain.reshape(1, -1) for gain in (q_gain, k_gain)]
    cube = is_cube(w_query.shape[0], local_cols) and w_out.shape[0] // owners % 16 == 0
    span_ids = owner_index * spans + jnp.arange(spans, dtype=jnp.int32)
    seen = (
        (window_mask == 1) & (span_ids[:, None] >= jnp.array([2, 1], jnp.int32)[None, :])
    ).astype(jnp.int32)

    if cube:
        mine = owner_index.astype(jnp.int32)
        high = w_query.shape[0]

        def indices(masks):
            return jnp.stack([mine ^ m for m in masks])

        halves_of = halves(w_query)
        sides = (jnp.concatenate([w_value, halves_of[0]]), jnp.concatenate([halves_of[1], w_key]))
        firsts = [{m: exchange(side, m) for m in (2, 4)} for side in sides]
        early, late = [0, 1, 2, 4, 3, 5], [6, 7]
        early_indices, late_indices = indices(early), indices(late)
        small = (seen, place, early_indices, late_indices, *gain_rows)
        normed = modulated_norm(after(latents, *small), control, levels, modulation, owners)
        firsts[0][4], firsts[1][2] = after(firsts[0][4], normed), after(firsts[1][2], normed)
        for side, first in zip(sides, firsts):
            first.update({0: side, 1: exchange(after(side, normed), 1)})
        share = out_shares(after(w_out, normed, firsts[0][4], firsts[1][2]))
        across = [
            exchange(after(firsts[0][4], normed, share), 2),
            exchange(after(firsts[1][2], normed, share), 4),
        ]
        firsts[0][2] = after(firsts[0][2], normed, share)
        firsts[1][4] = after(firsts[1][4], normed, share)
        firsts = [second_step(first) for first in firsts]
        columns = {"value": 0, "key": local_cols, "query": 2 * local_cols}
        half = high // 2

        def layout_of(count):
            return tuple(
                (
                    (2 * b, 0, high, 0, columns["value"]),
                    (2 * b, high, half, 0, columns["query"]),
                    (2 * b + 1, 0, half, half, columns["query"]),
                    (2 * b + 1, half, high, 0, columns["key"]),
                )
                for b in range(count)
            )

        parts = [first[m] for m in early for first in firsts]
        begun = project(normed, parts, layout_of(len(early)), early_indices, (3,))
        across = [after(part, begun) for part in across]
        parts = across + [exchange(part, 1) for part in across]
        own, query, squares = project(
            normed,
            parts,
            layout_of(len(late)),
            late_indices,
            (2, 1),
            begun=begun,
            spans=spans,
        )
    else:
        normed = modulated_norm(latents, control, levels, modulation, 1)
        weights = [
            lax.all_gather(w, "queue", axis=0, tiled=True) for w in (w_value, w_key, w_query)
        ]
        model = weights[0].shape[0]
        layout = (tuple((w, 0, model, 0, w * local_cols) for w in range(3)),)
        zero = jnp.zeros((1,), jnp.int32)
        own, query, squares = project(normed, weights, layout, zero, (2, 1), spans=spans)
        share = out_shares(w_out)

    prior = from_behind(own, "queue", 1)
    prior_squares = from_behind(squares, "queue", 1)
    share = out_blocks(after(share, prior_squares)) if cube else out_blocks(share)
    squares = sum_terms(jnp.concatenate([squares, prior_squares]), "head")

    def attended_of(span, ready):
        return attend(span, seen, ready, squares, gain_rows, prior, own, total_width)

    groups = lax.axis_size("head")
    attended_last = attended_of(spans - 1, query)
    last = along_line(attended_last, "head")
    sent = [last[1], last[groups]]
    begin_rest = [attended_last, *sent]
    if cube:
        share = after(share, *squares)
        first = {m: exchange(share, m) for m in (2, 4)}
    rest = [attended_of(span, after(query, *begin_rest)) for span in range(spans - 1)]
    rest = rest[0] if len(rest) == 1 else jnp.concatenate(rest, axis=0)
    line = along_line(rest, "head")
    if cube:
        first = {m: after(block, rest) for m, block in first.items()}
        half = share.shape[0] // 2
        across = [exchange(first[4][:half], 2), exchange(first[2][half:], 4)]
        across = jnp.concatenate([after(part, *last[1:]) for part in across])
        mine_blocks = jnp.stack([share, first[2], first[4], across])
        swapped = exchange(mine_blocks, 1)
        parts = [mine_blocks, swapped]
    else:
        weights = assemble_in_order(lax.all_gather(share, "queue", axis=0))
        parts = [weights]
    rest = line
    width = latents.shape[2] // groups
    updated_last = update_last(place, last, parts, latents, control, modulation, width)
    if cube:
        swapped = after(swapped, updated_last, rest[1], rest[groups])
        weights = assemble([mine_blocks, swapped], block_indices)
    arrived = shifted(updated_last, "queue", 1)
    return update_rest(place, arrived, rest, weights, latents, control, modulation)


def solution(mesh):
    placed = (
        P("queue", None, None),
        P("queue", None, None),
        P("queue"),
        P("queue", None),
        P(),
        P("queue", "head"),
        P("queue", "head"),
        P("queue", "head"),
        P("head", "queue"),
        P("head"),
        P("head"),
    )
    return jax.shard_map(
        shards, mesh=mesh, in_specs=placed, out_specs=P("queue", None, "head"), check_vma=False
    )
```
